512 devices in a mesh: lev: 8 (over x, z_lo), tile: 64 (over y, z_hi, core).
Axes of the slice: x: 4, y: 8, z: 8 (z_hi: 4, z_lo: 2; z = z_hi * 2 + z_lo), core: 2. Of those that a mesh axis runs over, the one named last changes fastest.
Arguments:
- thermal_deviation: float32 [64, 512, 4320], P('lev', 'tile'), may hold values from -6 to 6
- terrain_flag: int32 [512, 4320], P('tile'), may hold values 0 or 1
- frequency_share_limit_pointer: int32 [14], replicated, may hold values from 0 to 15
Outputs:
- coefficients: float32 [64, 512, 4320], P(None, 'tile', 'lev')
The draws below stay inside these ranges and needn't reach their ends.
All inputs are finite; a program needn't handle non-finite values. No bound on the sum of `terrain_flag` on one device may be relied on, other than what follows from the above.
Results may differ from the reference program's by a relative error of at most 0.0003.
Values sent between devices are 32-bit elements; how exact they have to be, the bound alone decides.
A program may use at most 64 MiB of HBM per device.

```python
import math
import jax
import jax.numpy as jnp
from jax import lax

STRATA_COUNT = 64
PANEL_STRIPES = 4320
BANDS = 14
TABLE = 16
PANEL_LINES = 512


def place_ends(values, stream_key, low, largest):
    longest = values.shape.index(max(values.shape))
    spots = []
    for shift in (0, 1):
        where = [jax.random.randint(jax.random.fold_in(stream_key, axis), (), 0, length) for axis, length in enumerate(values.shape)]
        where[longest] = (where[longest] + shift) % values.shape[longest]
        spots.append(tuple(where))
    return values.at[spots[0]].set(low).at[spots[1]].set(largest)


def block_levels(key, shape, cuts, low, top_value):
    gain, own = 1.0, jax.random.fold_in(key, 6)
    for position, blocks in cuts:
        heights = jnp.exp(jax.random.uniform(jax.random.fold_in(own, position), (blocks,), jnp.float32, low / len(cuts), top_value / len(cuts)))
        gain = gain * jnp.repeat(heights, shape[position] // blocks).reshape([-1 if axis == position else 1 for axis in range(len(shape))])
    return gain


def noise(stream_key, shape, scale, most, split=(), held_as=jnp.bfloat16):
    entries = jax.random.normal(stream_key, shape, jnp.float32) * scale
    if len(split) > 0:
        entries = block_levels(stream_key, shape, split, -0.22, 0.18) * entries
    return jnp.clip(entries, min=-most, max=most).astype(held_as)


def setup_inputs(seed: int = 0) -> dict:
    seeds = jax.random.split(jax.random.key(seed), 4)
    thermal_deviation = noise(seeds[0], (STRATA_COUNT, PANEL_LINES, PANEL_STRIPES), 1.0, 6.0, ((0, 8), (1, 64)), jnp.float32)
    terrain_flag = place_ends((jax.random.randint(seeds[1], (PANEL_LINES, PANEL_STRIPES), 0, 4) < 1).astype(jnp.int32), jax.random.fold_in(seeds[1], 1), 0, 1)
    frequency_share_limit_pointer = place_ends(jax.random.randint(seeds[2], (BANDS,), 0, TABLE), jax.random.fold_in(seeds[2], 1), 0, TABLE - 1).astype(jnp.int32)
    return dict(thermal_deviation=thermal_deviation, terrain_flag=terrain_flag, frequency_share_limit_pointer=frequency_share_limit_pointer)


ALPHA = -1.586134342
BETA = -0.05298011854
GAMMA = 0.8829110762
DELTA = 0.4435068522
KAPPA = 1.149604398

def cut_range(array, start, stop, dimension):
    return lax.slice_in_dim(array, start, stop, axis=dimension)

def lift_pairs(even_part, odd_part, dimension):
    total_pairs = even_part.shape[dimension]
    odd_one = cut_range(odd_part, 0, total_pairs - 1, dimension) + ALPHA * (cut_range(even_part, 0, total_pairs - 1, dimension) + cut_range(even_part, 1, total_pairs, dimension))
    even_two = cut_range(even_part, 1, total_pairs - 1, dimension) + BETA * (cut_range(odd_one, 0, total_pairs - 2, dimension) + cut_range(odd_one, 1, total_pairs - 1, dimension))
    odd_three = cut_range(odd_one, 1, total_pairs - 2, dimension) + GAMMA * (cut_range(even_two, 0, total_pairs - 3, dimension) + cut_range(even_two, 1, total_pairs - 2, dimension))
    even_four = cut_range(even_two, 1, total_pairs - 3, dimension) + DELTA * (cut_range(odd_three, 0, total_pairs - 4, dimension) + cut_range(odd_three, 1, total_pairs - 3, dimension))
    return (even_four / KAPPA, cut_range(odd_three, 1, total_pairs - 3, dimension) * KAPPA)

def lift_axis(mirrored_field, dimension):
    extent = mirrored_field.shape[dimension]
    even_part = lax.slice_in_dim(mirrored_field, 0, extent, stride=2, axis=dimension)
    odd_part = lax.slice_in_dim(mirrored_field, 1, extent, stride=2, axis=dimension)
    lowpass, highpass = lift_pairs(even_part, odd_part, dimension)
    low_config = [(0, 0, 0)] * 3
    high_config = [(0, 0, 0)] * 3
    low_config[dimension] = (0, 1, 1)
    high_config[dimension] = (1, 0, 1)
    zero = jnp.array(0.0, lowpass.dtype)
    return lax.pad(lowpass, zero, low_config) + lax.pad(highpass, zero, high_config)

def pad_columns(field):
    return jnp.pad(field, ((0, 0), (0, 0), (4, 4)))

def mirror_pad_rows(field):
    return jnp.pad(field, ((0, 0), (4, 4), (0, 0)))

def extract_coarse_band(field):
    return field[:, ::2, ::2]

def put_coarse(field, coarse):
    depth, height, width = field.shape
    zero = jnp.array(0.0, coarse.dtype)
    spread = lax.pad(coarse, zero, [(0, 0, 0), (0, 1, 1), (0, 1, 1)])
    row_iota = lax.broadcasted_iota(jnp.int32, (1, height, width), 1)
    col_iota = lax.broadcasted_iota(jnp.int32, (1, height, width), 2)
    corner = jnp.logical_and(row_iota % 2 == 0, col_iota % 2 == 0)
    return jnp.where(corner, spread, field)

def two_levels(field, columns_one, columns_two, rows_one, rows_two):
    field = lift_axis(columns_one(field), 2)
    field = lift_axis(rows_one(field), 1)
    coarse = extract_coarse_band(field)
    coarse = lift_axis(columns_two(coarse), 2)
    coarse = lift_axis(rows_two(coarse), 1)
    return put_coarse(field, coarse)

def d4_matrix(levels):
    root = math.sqrt(3.0)
    scale = 4.0 * math.sqrt(2.0)
    low_taps = [(1.0 + root) / scale, (3.0 + root) / scale, (3.0 - root) / scale, (1.0 - root) / scale]
    high_taps = [low_taps[3], -low_taps[2], low_taps[1], -low_taps[0]]
    half = levels // 2
    row_index = lax.broadcasted_iota(jnp.int32, (levels, levels), 0)
    col_index = lax.broadcasted_iota(jnp.int32, (levels, levels), 1)
    offset = (col_index - 2 * (row_index % half)) % levels
    matrix = jnp.zeros((levels, levels), jnp.float32)
    for tap_number in range(4):
        weight = jnp.where(row_index < half, low_taps[tap_number], high_taps[tap_number])
        matrix = matrix + jnp.where(offset == tap_number, weight, 0.0)
    return matrix.astype(jnp.float32)

def vertical_matrix(columns):
    levels = columns.shape[0]
    flat = columns.reshape(levels, -1)
    product = jnp.dot(d4_matrix(levels), flat, precision=lax.Precision.HIGHEST, preferred_element_type=jnp.float32)
    return product.reshape(columns.shape)

def threshold(coefs, frequency_share_limit_pointer):
    levels, height, width = coefs.shape
    cutoffs = (0.05 * 1.25 ** frequency_share_limit_pointer.astype(jnp.float32)).reshape(2, 7)
    row_iota = lax.broadcasted_iota(jnp.int32, (height, width), 0)
    col_iota = lax.broadcasted_iota(jnp.int32, (height, width), 1)
    row_odd = row_iota % 2
    col_odd = col_iota % 2
    fine_band = 3 + 2 * row_odd + col_odd
    coarse_band = 2 * (row_iota // 2 % 2) + col_iota // 2 % 2
    band = jnp.where(row_odd + col_odd > 0, fine_band, coarse_band)
    upper_cut = jnp.zeros((height, width), jnp.float32)
    lower_cut = jnp.zeros((height, width), jnp.float32)
    for band_number in range(7):
        upper_cut = jnp.where(band == band_number, cutoffs[0, band_number], upper_cut)
        lower_cut = jnp.where(band == band_number, cutoffs[1, band_number], lower_cut)
    level_iota = lax.broadcasted_iota(jnp.int32, (levels, 1, 1), 0)
    cutoff = jnp.where(level_iota < levels // 2, upper_cut[None], lower_cut[None])
    return jnp.sign(coefs) * jnp.maximum(jnp.abs(coefs) - cutoff, 0.0)

def reference(thermal_deviation, terrain_flag, frequency_share_limit_pointer):
    water_indicator = thermal_deviation * (1 - terrain_flag).astype(jnp.float32)[None]

    def per_level(plane):
        return two_levels(plane[None], pad_columns, pad_columns, mirror_pad_rows, mirror_pad_rows)[0]
    planar = lax.map(per_level, water_indicator)
    vertical = vertical_matrix(planar)
    return threshold(vertical, frequency_share_limit_pointer)
```

```python
import functools
import math

import jax
import jax.numpy as jnp
from jax import lax
from jax.experimental import pallas as pl
from jax.experimental.pallas import tpu as pltpu
from jax.sharding import PartitionSpec as P

ALPHA = -1.586134342
BETA = -0.05298011854
GAMMA = 0.8829110762
DELTA = 0.4435068522
KAPPA = 1.149604398

LANES = 128
ROWS = 8
WIDTH = 4320
PARTS = 8
BLOCK = WIDTH // PARTS
FULL = BLOCK // LANES
TAIL = BLOCK - FULL * LANES
SPAN = FULL + 1
PADDED = 36
MESH = pl.DeviceIdType.MESH


def row_messages(even, odd):
    first = odd[0] + ALPHA * (even[0] + even[1])
    before = odd[-2] + ALPHA * (even[-2] + even[-1])
    p = odd[-1] + ALPHA * even[-1]
    q = p + GAMMA * (even[-1] + BETA * (before + p))
    return (p, q), (even[0], first)


def row_lift(even, odd, p, q, r, s):
    n = len(even)
    odd_one = [p + ALPHA * even[0]]
    odd_one += [odd[j] + ALPHA * (even[j] + (even[j + 1] if j + 1 < n else r)) for j in range(n)]
    even_two = [even[j] + BETA * (odd_one[j] + odd_one[j + 1]) for j in range(n)]
    even_two.append(r + BETA * (odd_one[n] + s))
    odd_three = [q + (ALPHA * (1.0 + GAMMA * BETA)) * even[0] + GAMMA * even_two[0]]
    odd_three += [odd_one[j + 1] + GAMMA * (even_two[j] + even_two[j + 1]) for j in range(n)]
    even_four = [even_two[j] + DELTA * (odd_three[j] + odd_three[j + 1]) for j in range(n)]
    return even_four, odd_three[1:]


def turn(value, amount):
    return pltpu.roll(value, amount % LANES, axis=1)


def column_lift(even, odd, step, lane):
    n = len(even)

    def following(tiles):
        rolled = [turn(v, -step) for v in tiles]
        return [jnp.where(lane >= LANES - step, rolled[(j + 1) % n], rolled[j]) for j in range(n)]

    def preceding(tiles):
        rolled = [turn(v, step) for v in tiles]
        return [jnp.where(lane < step, rolled[j - 1], rolled[j]) for j in range(n)]

    odd = [o + ALPHA * (e + f) for o, e, f in zip(odd, even, following(even))]
    even = [e + BETA * (o + f) for e, o, f in zip(even, odd, preceding(odd))]
    odd = [o + GAMMA * (e + f) for o, e, f in zip(odd, even, following(even))]
    even = [e + DELTA * (o + f) for e, o, f in zip(even, odd, preceding(odd))]
    return even, odd


def split_pair(a, b, step, keep):
    even = [jnp.where(keep, u, turn(v, step)) for u, v in zip(a, b)]
    odd = [jnp.where(keep, turn(u, -step), v) for u, v in zip(a, b)]
    return even, odd


def join_pair(even, odd, step, keep):
    a = [jnp.where(keep, e, turn(o, step)) for e, o in zip(even, odd)]
    b = [jnp.where(keep, turn(e, -step), o) for e, o in zip(even, odd)]
    return a, b


def tap_values():
    root = math.sqrt(3.0)
    scale = 4.0 * math.sqrt(2.0)
    low = [(1.0 + root) / scale, (3.0 + root) / scale, (3.0 - root) / scale, (1.0 - root) / scale]
    return low, [low[3], -low[2], low[1], -low[0]]


def cutoff_pattern(pointer_ref, half):
    row = lax.broadcasted_iota(jnp.int32, (ROWS, LANES), 0)
    col = lax.broadcasted_iota(jnp.int32, (ROWS, LANES), 1)
    fine = 3 + 2 * (row % 2) + col % 2
    coarse = 2 * (row // 2 % 2) + col // 2 % 2
    band = jnp.where(row % 2 + col % 2 > 0, fine, coarse)
    power = jnp.zeros((ROWS, LANES), jnp.int32)
    for number in range(7):
        power = jnp.where(band == number, pointer_ref[7 * half + number], power)
    cutoff = jnp.full((ROWS, LANES), 0.05, jnp.float32)
    for bit in range(4):
        factor = 1.25 ** (2**bit)
        cutoff = jnp.where((power // 2**bit) % 2 == 1, cutoff * factor, cutoff)
    return cutoff


def kernel(
    tiles_count,
    x_ref,
    flag_ref,
    pointer_ref,
    out_ref,
    field,
    to_next,
    to_prev,
    from_prev,
    from_next,
    window,
    hold,
    to_next2,
    to_prev2,
    from_prev2,
    from_next2,
    send_main,
    send_tail,
    recv_main,
    recv_tail,
    levels,
    edge_send,
    edge_recv,
    edge2_send,
    edge2_recv,
    main_send,
    main_recv,
    tail_send,
    tail_recv,
    own_sem,
):
    me = lax.axis_index("lev")
    row_block = lax.axis_index("tile")
    has_prev = row_block > 0
    has_next = row_block < tiles_count - 1
    lane = lax.broadcasted_iota(jnp.int32, (ROWS, LANES), 1)
    lane_even = lane % 2 == 0
    lane_low = lane % 4 < 2
    nothing = jnp.zeros((ROWS, LANES), jnp.float32)

    barrier = pltpu.get_barrier_semaphore()
    for step in range(1, PARTS):
        pl.semaphore_signal(
            barrier,
            inc=1,
            device_id={"lev": lax.rem(me + step, PARTS)},
            device_id_type=MESH,
        )

    @pl.when(has_prev)
    def _():
        pl.semaphore_signal(
            barrier, inc=1, device_id={"tile": row_block - 1}, device_id_type=MESH
        )

    @pl.when(has_next)
    def _():
        pl.semaphore_signal(
            barrier, inc=1, device_id={"tile": row_block + 1}, device_id_type=MESH
        )

    field[pl.ds(0, ROWS * ROWS), :] = jnp.zeros((ROWS * ROWS, LANES), jnp.float32)
    field[pl.ds((PADDED - 2) * ROWS * ROWS, 2 * ROWS * ROWS), :] = jnp.zeros(
        (2 * ROWS * ROWS, LANES), jnp.float32
    )
    last = WIDTH // LANES
    rest = WIDTH - last * LANES

    def load_tile(tile, _):
        columns = pl.ds(pl.multiple_of(tile * LANES, LANES), LANES)
        water = (1 - flag_ref[:, columns]).astype(jnp.float32)
        for level in range(ROWS):
            start = pl.multiple_of((tile + 1) * ROWS * ROWS + level * ROWS, ROWS)
            field[pl.ds(start, ROWS), :] = x_ref[level, :, columns] * water
        return 0

    lax.fori_loop(0, last, load_tile, 0)
    water = (1 - flag_ref[:, pl.ds(last * LANES, rest)]).astype(jnp.float32)
    for level in range(ROWS):
        start = (last + 1) * ROWS * ROWS + level * ROWS
        field[pl.ds(start, ROWS), pl.ds(0, rest)] = (
            x_ref[level, :, pl.ds(last * LANES, rest)] * water
        )

    def rows_of(tile):
        return [
            field[pl.ds(tile * ROWS * ROWS + row, ROWS, stride=ROWS), :] for row in range(ROWS)
        ]

    def edge_tile(tile, _):
        rows = rows_of(tile)
        forward, backward = row_messages(rows[0::2], rows[1::2])
        for i in range(2):
            to_next[tile, i] = forward[i]
            to_prev[tile, i] = backward[i]
        return 0

    lax.fori_loop(1, PADDED - 1, edge_tile, 0)

    for ref in (from_prev, from_next):
        for tile in (0, PADDED - 1):
            for i in range(2):
                ref[tile, i] = nothing

    def clear(edge, edge2):
        def clear_tile(tile, _):
            for i in range(2):
                edge[tile, i] = nothing
            return 0

        def clear_second(k, _):
            for j in range(SPAN):
                edge2[k, j] = nothing
            return 0

        lax.fori_loop(1, PADDED - 1, clear_tile, 0)
        lax.fori_loop(0, PARTS, clear_second, 0)

    @pl.when(jnp.logical_not(has_prev))
    def _():
        clear(from_prev, from_prev2)

    @pl.when(jnp.logical_not(has_next))
    def _():
        clear(from_next, from_next2)

    pl.semaphore_wait(
        barrier, PARTS - 1 + jnp.where(has_prev, 1, 0) + jnp.where(has_next, 1, 0)
    )

    body = pl.ds(1, PADDED - 2)

    def edge_forward():
        return pltpu.make_async_remote_copy(
            src_ref=to_next.at[body],
            dst_ref=from_prev.at[body],
            send_sem=edge_send.at[0],
            recv_sem=edge_recv.at[0],
            device_id={"tile": row_block + 1},
            device_id_type=MESH,
        )

    def edge_backward():
        return pltpu.make_async_remote_copy(
            src_ref=to_prev.at[body],
            dst_ref=from_next.at[body],
            send_sem=edge_send.at[1],
            recv_sem=edge_recv.at[1],
            device_id={"tile": row_block - 1},
            device_id_type=MESH,
        )

    def edge2_forward(k):
        return pltpu.make_async_remote_copy(
            src_ref=to_next2.at[k],
            dst_ref=from_prev2.at[k],
            send_sem=edge2_send.at[0, k],
            recv_sem=edge2_recv.at[0, k],
            device_id={"tile": row_block + 1},
            device_id_type=MESH,
        )

    def edge2_backward(k):
        return pltpu.make_async_remote_copy(
            src_ref=to_prev2.at[k],
            dst_ref=from_next2.at[k],
            send_sem=edge2_send.at[1, k],
            recv_sem=edge2_recv.at[1, k],
            device_id={"tile": row_block - 1},
            device_id_type=MESH,
        )

    def target(k):
        return lax.rem(me + 1 + k, PARTS)

    def main_copy(k, parity):
        return pltpu.make_async_remote_copy(
            src_ref=send_main.at[k, :, parity],
            dst_ref=recv_main.at[me, :, parity],
            send_sem=main_send.at[parity, k],
            recv_sem=main_recv.at[parity, k],
            device_id={"lev": target(k)},
            device_id_type=MESH,
        )

    def tail_copy(k):
        return pltpu.make_async_remote_copy(
            src_ref=send_tail.at[k],
            dst_ref=recv_tail.at[me],
            send_sem=tail_send.at[k],
            recv_sem=tail_recv.at[k],
            device_id={"lev": target(k)},
            device_id_type=MESH,
        )

    own = PARTS - 1

    def own_main(parity):
        return pltpu.make_async_copy(
            send_main.at[own, :, parity], recv_main.at[me, :, parity], own_sem.at[parity]
        )

    def own_tail():
        return pltpu.make_async_copy(send_tail.at[own], recv_tail.at[me], own_sem.at[2])

    @pl.when(has_next)
    def _():
        edge_forward().start()

    @pl.when(has_prev)
    def _():
        edge_backward().start()

    @pl.when(has_prev)
    def _():
        edge_forward().wait_recv()

    @pl.when(has_next)
    def _():
        edge_backward().wait_recv()

    def put_rows(k, parity, rows):
        tail = rows[0][FULL]
        for i in range(4):
            for j in range(FULL):
                send_main[k, i, parity, pl.ds(j * ROWS, ROWS), :] = rows[i][j]
            if i > 0:
                tail = jnp.where(lane >= i * TAIL, turn(rows[i][FULL], i * TAIL), tail)
        send_tail[k, parity] = tail

    def first_stage(k, _):
        block = target(k)
        first = (block * BLOCK) // LANES
        shift = block * BLOCK - first * LANES
        back = lax.rem(LANES - shift, LANES)
        inside = lane < LANES - shift
        for i in range(SPAN + 2):
            rows = rows_of(first + i)
            even, odd = row_lift(
                rows[0::2],
                rows[1::2],
                from_prev[first + i, 0],
                from_prev[first + i, 1],
                from_next[first + i, 0],
                from_next[first + i, 1],
            )
            for j in range(4):
                window[2 * j, i] = pltpu.roll(even[j], back, axis=1)
                window[2 * j + 1, i] = pltpu.roll(odd[j], back, axis=1)

        def aligned(row):
            tiles = [window[row, i] for i in range(SPAN + 2)]
            moved = [jnp.where(inside, tiles[i], tiles[i + 1]) for i in range(SPAN + 1)]
            return moved[1:SPAN] + [jnp.where(lane < LANES // 2, moved[SPAN], moved[0])]

        def lifted(a, b):
            even, odd = split_pair(aligned(a), aligned(b), 1, lane_even)
            return column_lift(even, odd, 1 * 2, lane)

        rows = [None] * ROWS
        for a, b in ((1, 5), (3, 7)):
            even, odd = lifted(a, b)
            odd = [v * (KAPPA * KAPPA) for v in odd]
            rows[a], rows[b] = join_pair(even, odd, 1, lane_even)
        put_rows(k, 1, rows[1::2])

        @pl.when(k < own)
        def _():
            main_copy(k, 1).start()

        @pl.when(k == own)
        def _():
            own_main(1).start()

        within = jnp.logical_or(
            lane < TAIL,
            jnp.logical_or(
                jnp.logical_and(lane < LANES // 2, block < PARTS - 1),
                jnp.logical_and(lane >= LANES // 2, block > 0),
            ),
        )
        low_a, high_a = lifted(0, 4)
        low_b, high_b = lifted(2, 6)
        low_a[FULL] = jnp.where(within, low_a[FULL], 0.0)
        low_b[FULL] = jnp.where(within, low_b[FULL], 0.0)
        even, odd = split_pair(low_a, low_b, 2, lane_low)
        even, odd = column_lift(even, odd, 4, lane)
        low_a, low_b = join_pair(even, odd, 2, lane_low)
        c0, c2 = join_pair(low_a, high_a, 1, lane_even)
        c1, c3 = join_pair(low_b, high_b, 1, lane_even)
        for j in range(SPAN):
            for i, row in enumerate((c0, c1, c2, c3)):
                hold[k, i, j] = row[j]
            (p, q), (r, s) = row_messages([c0[j], c2[j]], [c1[j], c3[j]])
            to_next2[k, j] = jnp.where(lane_even, p, turn(q, 1))
            to_prev2[k, j] = jnp.where(lane_even, r, turn(s, 1))

        @pl.when(has_next)
        def _():
            edge2_forward(k).start()

        @pl.when(has_prev)
        def _():
            edge2_backward(k).start()

        return 0

    lax.fori_loop(0, PARTS, first_stage, 0)

    square = KAPPA * KAPPA
    one = jnp.ones((ROWS, LANES), jnp.float32)
    scale_even = jnp.where(
        lane_even, jnp.where(lane_low, 1.0 / (square * square), 1.0 / square), one
    )
    scale_odd = jnp.where(jnp.logical_and(lane_even, lane_low), 1.0 / square, one)

    def second_stage(k, _):
        @pl.when(has_prev)
        def _():
            edge2_forward(k).wait_recv()

        @pl.when(has_next)
        def _():
            edge2_backward(k).wait_recv()

        rows = [[None] * SPAN for _ in range(4)]
        for j in range(SPAN):
            c = [hold[k, i, j] for i in range(4)]
            p = from_prev2[k, j]
            r = from_next2[k, j]
            even, odd = row_lift(c[0::2], c[1::2], p, turn(p, -1), r, turn(r, -1))
            for i in range(2):
                rows[2 * i][j] = jnp.where(lane_even, even[i], c[2 * i]) * scale_even
                rows[2 * i + 1][j] = jnp.where(lane_even, odd[i], c[2 * i + 1]) * scale_odd
        put_rows(k, 0, rows)

        @pl.when(k < own)
        def _():
            main_copy(k, 0).start()
            tail_copy(k).start()

        @pl.when(k == own)
        def _():
            own_main(0).start()
            own_tail().start()

        return 0

    lax.fori_loop(0, PARTS, second_stage, 0)

    own_main(1).wait()
    own_main(0).wait()
    own_tail().wait()

    def arrived(k, _):
        main_copy(k, 1).wait_recv()
        main_copy(k, 0).wait_recv()
        tail_copy(k).wait_recv()
        return 0

    lax.fori_loop(0, own, arrived, 0)

    def spread(source, _):
        for parity in range(2):
            tail = recv_tail[source, parity]
            for i in range(4):
                start = ((source * ROWS + 2 * i + parity) * SPAN) * ROWS
                for j in range(FULL):
                    levels[pl.ds(pl.multiple_of(start + j * ROWS, ROWS), ROWS), :] = recv_main[
                        source, i, parity, pl.ds(j * ROWS, ROWS), :
                    ]
                levels[pl.ds(pl.multiple_of(start + FULL * ROWS, ROWS), ROWS), :] = turn(
                    tail, -i * TAIL
                )
        return 0

    lax.fori_loop(0, PARTS, spread, 0)

    low_taps, high_taps = tap_values()
    cutoffs = [cutoff_pattern(pointer_ref, half) for half in range(2)]

    def level_tile(source, level, j):
        start = source * ROWS * SPAN * ROWS + j * ROWS + level
        return levels[pl.ds(start, ROWS, stride=SPAN * ROWS), :]

    def vertical(source, _):
        after = lax.rem(source + 1, PARTS)
        for j in range(SPAN):
            taken = [level_tile(source, level, j) for level in range(ROWS)]
            taken += [level_tile(after, level, j) for level in range(2)]
            for i in range(ROWS // 2):
                for half, taps in enumerate((low_taps, high_taps)):
                    value = taps[0] * taken[2 * i]
                    for tap in range(1, 4):
                        value = value + taps[tap] * taken[2 * i + tap]
                    cutoff = cutoffs[half]
                    value = value - jnp.minimum(jnp.maximum(value, -cutoff), cutoff)
                    row = half * PARTS * ROWS // 2 + source * (ROWS // 2) + i
                    if j == FULL:
                        out_ref[row, :, pl.ds(FULL * LANES, TAIL)] = value[:, :TAIL]
                    else:
                        out_ref[row, :, pl.ds(j * LANES, LANES)] = value
        return 0

    lax.fori_loop(0, PARTS, vertical, 0)

    @pl.when(has_next)
    def _():
        edge_forward().wait_send()

    @pl.when(has_prev)
    def _():
        edge_backward().wait_send()

    def sent(k, _):
        @pl.when(has_next)
        def _():
            edge2_forward(k).wait_send()

        @pl.when(has_prev)
        def _():
            edge2_backward(k).wait_send()

        @pl.when(k < own)
        def _():
            main_copy(k, 1).wait_send()
            main_copy(k, 0).wait_send()
            tail_copy(k).wait_send()

        return 0

    lax.fori_loop(0, PARTS, sent, 0)


def local(tiles_count, thermal_deviation, terrain_flag, frequency_share_limit_pointer):
    tile = (ROWS, LANES)
    vmem = lambda *shape: pltpu.VMEM(shape, jnp.float32)
    dma = pltpu.SemaphoreType.DMA
    return pl.pallas_call(
        functools.partial(kernel, tiles_count),
        out_shape=jax.ShapeDtypeStruct((PARTS * ROWS, ROWS, BLOCK), jnp.float32),
        in_specs=[
            pl.BlockSpec(memory_space=pltpu.VMEM),
            pl.BlockSpec(memory_space=pltpu.VMEM),
            pl.BlockSpec(memory_space=pltpu.SMEM),
        ],
        out_specs=pl.BlockSpec(memory_space=pltpu.VMEM),
        scratch_shapes=[
            vmem(PADDED * ROWS * ROWS, LANES),
            vmem(PADDED, 2, *tile),
            vmem(PADDED, 2, *tile),
            vmem(PADDED, 2, *tile),
            vmem(PADDED, 2, *tile),
            vmem(ROWS, SPAN + 2, *tile),
            vmem(PARTS, 4, SPAN, *tile),
            vmem(PARTS, SPAN, *tile),
            vmem(PARTS, SPAN, *tile),
            vmem(PARTS, SPAN, *tile),
            vmem(PARTS, SPAN, *tile),
            vmem(PARTS, 4, 2, FULL * ROWS, LANES),
            vmem(PARTS, 2, *tile),
            vmem(PARTS, 4, 2, FULL * ROWS, LANES),
            vmem(PARTS, 2, *tile),
            vmem(PARTS * ROWS * SPAN * ROWS, LANES),
            dma((2,)),
            dma((2,)),
            dma((2, PARTS)),
            dma((2, PARTS)),
            dma((2, PARTS)),
            dma((2, PARTS)),
            dma((PARTS,)),
            dma((PARTS,)),
            dma((3,)),
        ],
        compiler_params=pltpu.CompilerParams(
            collective_id=0, has_side_effects=True, vmem_limit_bytes=32 * 1024 * 1024
        ),
    )(thermal_deviation, terrain_flag, frequency_share_limit_pointer)


def solution(mesh):
    placed = (P("lev", "tile", None), P("tile", None), P())
    return jax.shard_map(
        functools.partial(local, mesh.shape["tile"]),
        mesh=mesh,
        in_specs=placed,
        out_specs=P(None, "tile", "lev"),
        check_vma=False,
    )
```

```python
import functools
import math

import jax
import jax.numpy as jnp
import numpy as np
from jax import lax
from jax.experimental import pallas as pl
from jax.experimental.pallas import tpu as pltpu
from jax.sharding import PartitionSpec as P

ALPHA = -1.586134342
BETA = -0.05298011854
GAMMA = 0.8829110762
DELTA = 0.4435068522
KAPPA = 1.149604398

LANES = 128
ROWS = 8
WIDTH = 4320
PARTS = 8
BLOCK = WIDTH // PARTS
FULL = BLOCK // LANES
TAIL = BLOCK - FULL * LANES
SPAN = FULL + 1
WINDOWS = 4
WIDE = 9
LAST = 2 * BLOCK - (WIDE - 1) * LANES
HALO = (LANES - LAST) // 2
PADDED = 36
GROUP = ROWS * ROWS
ROW_LINES = FULL * ROWS
SLOTS = (3, 5, 7, 1, 0, 2, 4, 6)
ROW_AT = {row: i * ROW_LINES for i, row in enumerate(SLOTS)}
ODD_TAILS = ROWS * ROW_LINES
EVEN_TAILS = ODD_TAILS + ROWS
MESSAGE = EVEN_TAILS + ROWS
PIECES = (
    (0, ROW_LINES),
    (ROW_LINES, 2 * ROW_LINES),
    (3 * ROW_LINES, ROW_LINES),
    (4 * ROW_LINES, MESSAGE - 4 * ROW_LINES),
)
TAIL_AT = {row: row // 2 for row in range(ROWS)}
CHAIN = 8
MESH = pl.DeviceIdType.MESH


def impulse_responses():
    low, high = [], []
    for distance in range(5):
        for centre, taps in ((16, low), (17, high)):
            signal = np.zeros(34)
            signal[centre + distance] = 1.0
            even, odd = signal[0::2].copy(), signal[1::2].copy()
            odd[:-1] += ALPHA * (even[:-1] + even[1:])
            even[1:] += BETA * (odd[:-1] + odd[1:])
            odd[:-1] += GAMMA * (even[:-1] + even[1:])
            even[1:] += DELTA * (odd[:-1] + odd[1:])
            taps.append(float(even[8] if centre == 16 else odd[8]))
    return low, high[:4]


LOW, HIGH = impulse_responses()


def row_messages(even, odd):
    first = odd[0] + ALPHA * (even[0] + even[1])
    before = odd[-2] + ALPHA * (even[-2] + even[-1])
    p = odd[-1] + ALPHA * even[-1]
    q = p + GAMMA * (even[-1] + BETA * (before + p))
    return (p, q), (even[0], first)


def row_lift(even, odd, p, q, r, s):
    n = len(even)
    odd_one = [p + ALPHA * even[0]]
    odd_one += [odd[j] + ALPHA * (even[j] + (even[j + 1] if j + 1 < n else r)) for j in range(n)]
    even_two = [even[j] + BETA * (odd_one[j] + odd_one[j + 1]) for j in range(n)]
    even_two.append(r + BETA * (odd_one[n] + s))
    odd_three = [q + (ALPHA * (1.0 + GAMMA * BETA)) * even[0] + GAMMA * even_two[0]]
    odd_three += [odd_one[j + 1] + GAMMA * (even_two[j] + even_two[j + 1]) for j in range(n)]
    even_four = [even_two[j] + DELTA * (odd_three[j] + odd_three[j + 1]) for j in range(n)]
    return even_four, odd_three[1:]


def turn(value, amount):
    return pltpu.roll(value, amount % LANES, axis=1)


def column_lift(even, odd, step, lane, high_scale=1.0):
    n = len(even)

    def moved(tiles, distance):
        lanes = distance * step
        rolled = [turn(v, -lanes) for v in tiles]
        if distance > 0:
            return [jnp.where(lane >= LANES - lanes, rolled[(j + 1) % n], rolled[j]) for j in range(n)]
        return [jnp.where(lane < -lanes, rolled[j - 1], rolled[j]) for j in range(n)]

    even_at = {d: moved(even, d) for d in (-2, -1, 1, 2)}
    odd_at = {d: moved(odd, d) for d in (-2, -1, 1)}
    high_taps = [high_scale * tap for tap in HIGH]
    low, high = [], []
    for j in range(n):
        low.append(
            LOW[0] * even[j]
            + LOW[1] * (odd_at[-1][j] + odd[j])
            + LOW[2] * (even_at[-1][j] + even_at[1][j])
            + LOW[3] * (odd_at[-2][j] + odd_at[1][j])
            + LOW[4] * (even_at[-2][j] + even_at[2][j])
        )
        high.append(
            high_taps[0] * odd[j]
            + high_taps[1] * (even[j] + even_at[1][j])
            + high_taps[2] * (odd_at[-1][j] + odd_at[1][j])
            + high_taps[3] * (even_at[-1][j] + even_at[2][j])
        )
    return low, high


def split_pair(a, b, step, keep):
    even = [jnp.where(keep, u, turn(v, step)) for u, v in zip(a, b)]
    odd = [jnp.where(keep, turn(u, -step), v) for u, v in zip(a, b)]
    return even, odd


def join_pair(even, odd, step, keep):
    a = [jnp.where(keep, e, turn(o, step)) for e, o in zip(even, odd)]
    b = [jnp.where(keep, turn(e, -step), o) for e, o in zip(even, odd)]
    return a, b


def tap_values():
    root = math.sqrt(3.0)
    scale = 4.0 * math.sqrt(2.0)
    low = [(1.0 + root) / scale, (3.0 + root) / scale, (3.0 - root) / scale, (1.0 - root) / scale]
    return low, [low[3], -low[2], low[1], -low[0]]


def cutoff_pattern(pointer_ref, half):
    row = lax.broadcasted_iota(jnp.int32, (ROWS, LANES), 0)
    col = lax.broadcasted_iota(jnp.int32, (ROWS, LANES), 1)
    fine = 3 + 2 * (row % 2) + col % 2
    coarse = 2 * (row // 2 % 2) + col // 2 % 2
    band = jnp.where(row % 2 + col % 2 > 0, fine, coarse)
    power = jnp.zeros((ROWS, LANES), jnp.int32)
    for number in range(7):
        power = jnp.where(band == number, pointer_ref[7 * half + number], power)
    cutoff = jnp.full((ROWS, LANES), 0.05, jnp.float32)
    for bit in range(4):
        factor = 1.25 ** (2**bit)
        cutoff = jnp.where((power // 2**bit) % 2 == 1, cutoff * factor, cutoff)
    return cutoff


def kernel(
    tiles_count,
    x_hbm,
    flag_hbm,
    pointer_ref,
    out_hbm,
    out_ref,
    x_ref,
    flag_ref,
    field,
    aligned,
    to_next,
    to_prev,
    from_prev,
    from_next,
    window,
    hold,
    to_next2,
    to_prev2,
    from_prev2,
    from_next2,
    send,
    recv,
    levels,
    load_sem,
    edge_send,
    edge_recv,
    edge2_send,
    edge2_recv,
    block_send,
    block_recv,
    own_sem,
    store_sem,
    ready,
):
    me = lax.axis_index("lev")
    row_block = lax.axis_index("tile")
    place, half = me // 2, lax.rem(me, 2)
    has_prev = row_block > 0
    has_next = row_block < tiles_count - 1
    seam_prev = lax.rem(row_block, CHAIN) == 0
    seam_next = lax.rem(row_block, CHAIN) == CHAIN - 1
    early_prev = jnp.logical_and(has_prev, jnp.logical_not(seam_prev))
    late_prev = jnp.logical_and(has_prev, seam_prev)
    early_next = jnp.logical_and(has_next, seam_next)
    late_next = jnp.logical_and(has_next, jnp.logical_not(seam_next))
    row_1_first = lax.rem(row_block, CHAIN) == 1
    lane = lax.broadcasted_iota(jnp.int32, (ROWS, LANES), 1)
    lane_even = lane % 2 == 0
    lane_low = lane % 4 < 2
    nothing = jnp.zeros((ROWS, LANES), jnp.float32)

    barrier = pltpu.get_barrier_semaphore()
    for step in range(1, PARTS):
        pl.semaphore_signal(
            barrier,
            inc=1,
            device_id={"lev": lax.rem(me + step, PARTS)},
            device_id_type=MESH,
        )

    @pl.when(late_prev)
    def _():
        pl.semaphore_signal(
            barrier, inc=1, device_id={"tile": row_block - 1}, device_id_type=MESH
        )

    @pl.when(late_next)
    def _():
        pl.semaphore_signal(
            barrier, inc=1, device_id={"tile": row_block + 1}, device_id_type=MESH
        )

    loads = [
        pltpu.make_async_copy(x_hbm.at[level], x_ref.at[level], load_sem.at[level])
        for level in range(ROWS)
    ]
    loads.append(pltpu.make_async_copy(flag_hbm, flag_ref, load_sem.at[ROWS]))
    for load in loads:
        load.start()

    def clear(edge, edge2):
        def clear_window(k, _):
            for j in range(WIDE):
                edge[k, j, 0] = nothing
                edge[k, j, 1] = nothing
                edge2[k, j] = nothing
            return 0

        lax.fori_loop(0, WINDOWS, clear_window, 0)

    @pl.when(jnp.logical_not(has_prev))
    def _():
        clear(from_prev, from_prev2)

    @pl.when(jnp.logical_not(has_next))
    def _():
        clear(from_next, from_next2)

    field[pl.ds(0, GROUP), :] = jnp.zeros((GROUP, LANES), jnp.float32)
    field[pl.ds((PADDED - 2) * GROUP, 2 * GROUP), :] = jnp.zeros((2 * GROUP, LANES), jnp.float32)
    pl.semaphore_wait(
        barrier, PARTS - 1 + jnp.where(early_prev, 1, 0) + jnp.where(early_next, 1, 0)
    )

    @pl.when(early_prev)
    def _():
        pl.semaphore_signal(
            ready.at[0], inc=1, device_id={"tile": row_block - 1}, device_id_type=MESH
        )

    @pl.when(early_next)
    def _():
        pl.semaphore_signal(
            ready.at[1], inc=1, device_id={"tile": row_block + 1}, device_id_type=MESH
        )

    for load in loads:
        load.wait()

    whole = WIDTH // LANES
    rest = WIDTH - whole * LANES

    def load_tile(tile, _):
        columns = pl.ds(pl.multiple_of(tile * LANES, LANES), LANES)
        water = (1 - flag_ref[:, columns]).astype(jnp.float32)
        for level in range(ROWS):
            start = pl.multiple_of((tile + 1) * GROUP + level * ROWS, ROWS)
            field[pl.ds(start, ROWS), :] = x_ref[level, :, columns] * water
        return 0

    lax.fori_loop(0, whole, load_tile, 0)
    water = (1 - flag_ref[:, pl.ds(whole * LANES, rest)]).astype(jnp.float32)
    for level in range(ROWS):
        start = (whole + 1) * GROUP + level * ROWS
        field[pl.ds(start, ROWS), pl.ds(0, rest)] = (
            x_ref[level, :, pl.ds(whole * LANES, rest)] * water
        )

    def window_of(k):
        return lax.rem(place + 1 + k, WINDOWS)

    def edge_forward(k):
        return pltpu.make_async_remote_copy(
            src_ref=to_next.at[k],
            dst_ref=from_prev.at[k],
            send_sem=edge_send.at[0, k],
            recv_sem=edge_recv.at[0, k],
            device_id={"tile": row_block + 1},
            device_id_type=MESH,
        )

    def edge_backward(k):
        return pltpu.make_async_remote_copy(
            src_ref=to_prev.at[k],
            dst_ref=from_next.at[k],
            send_sem=edge_send.at[1, k],
            recv_sem=edge_recv.at[1, k],
            device_id={"tile": row_block - 1},
            device_id_type=MESH,
        )

    def edge2_forward(k):
        return pltpu.make_async_remote_copy(
            src_ref=to_next2.at[k],
            dst_ref=from_prev2.at[k],
            send_sem=edge2_send.at[0, k],
            recv_sem=edge2_recv.at[0, k],
            device_id={"tile": row_block + 1},
            device_id_type=MESH,
        )

    def edge2_backward(k):
        return pltpu.make_async_remote_copy(
            src_ref=to_prev2.at[k],
            dst_ref=from_next2.at[k],
            send_sem=edge2_send.at[1, k],
            recv_sem=edge2_recv.at[1, k],
            device_id={"tile": row_block - 1},
            device_id_type=MESH,
        )

    def block_copy(k, b, piece):
        lines = pl.ds(*PIECES[piece])
        return pltpu.make_async_remote_copy(
            src_ref=send.at[2 * k + b, lines],
            dst_ref=recv.at[me, lines],
            send_sem=block_send.at[piece, 2 * k + b],
            recv_sem=block_recv.at[piece, me],
            device_id={"lev": 2 * window_of(k) + b},
            device_id_type=MESH,
        )

    def from_source(source, piece):
        lines = pl.ds(*PIECES[piece])
        return pltpu.make_async_remote_copy(
            src_ref=send.at[0, lines],
            dst_ref=recv.at[source, lines],
            send_sem=block_send.at[piece, 0],
            recv_sem=block_recv.at[piece, source],
            device_id={"lev": source},
            device_id_type=MESH,
        )

    def own_copy(piece):
        lines = pl.ds(*PIECES[piece])
        return pltpu.make_async_copy(
            send.at[2 * (WINDOWS - 1) + half, lines], recv.at[me, lines], own_sem.at[piece]
        )

    def start_blocks(k, piece):
        for b in range(2):
            is_own = jnp.logical_and(k == WINDOWS - 1, half == b)

            @pl.when(jnp.logical_not(is_own))
            def _():
                block_copy(k, b, piece).start()

            @pl.when(is_own)
            def _():
                own_copy(piece).start()

    def put_row(k, row, tiles, first=False):
        at = ROW_AT[row]
        for j in range(FULL):
            send[2 * k, pl.ds(at + j * ROWS, ROWS), :] = tiles[j]
        rolled = [turn(tiles[j], -TAIL) for j in range(FULL, WIDE)]
        for j in range(FULL):
            send[2 * k + 1, pl.ds(at + j * ROWS, ROWS), :] = jnp.where(
                lane < LANES - TAIL, rolled[j], rolled[j + 1]
            )
        start = TAIL * TAIL_AT[row]
        lines = pl.ds(ODD_TAILS if row % 2 else EVEN_TAILS, ROWS)
        for b, tail in enumerate((tiles[FULL], rolled[FULL])):
            tail = turn(tail, start)
            if not first:
                mine = jnp.logical_and(lane >= start, lane < start + TAIL)
                tail = jnp.where(mine, tail, send[2 * k + b, lines, :])
            send[2 * k + b, lines, :] = tail

    def rows_of(k, j):
        start = (k * WIDE + j) * GROUP
        return [aligned[pl.ds(start + row, ROWS, stride=ROWS), :] for row in range(ROWS)]

    def edge_stage(k, _):
        w = window_of(k)
        first = (w * 2 * BLOCK) // LANES
        shift = w * 2 * BLOCK - first * LANES
        back = lax.rem(LANES - shift, LANES)
        inside = lane < LANES - shift
        halo, before = None, None
        for i in range(WIDE + 2):
            tile = [
                pltpu.roll(
                    field[pl.ds(pl.multiple_of((first + i) * GROUP + level * ROWS, ROWS), ROWS), :],
                    back,
                    axis=1,
                )
                for level in range(ROWS)
            ]
            if i > 0:
                moved = [jnp.where(inside, u, v) for u, v in zip(before, tile)]
                if i == 1:
                    halo = moved
                else:
                    if i == WIDE + 1:
                        moved = [
                            jnp.where(lane < LAST + HALO, u, v) for u, v in zip(moved, halo)
                        ]
                    for level in range(ROWS):
                        start = (k * WIDE + i - 2) * GROUP + level * ROWS
                        aligned[pl.ds(pl.multiple_of(start, ROWS), ROWS), :] = moved[level]
            before = tile
        for j in range(WIDE):
            rows = rows_of(k, j)
            forward, backward = row_messages(rows[0::2], rows[1::2])
            for i in range(2):
                to_next[k, j, i] = forward[i]
                to_prev[k, j, i] = backward[i]

        @pl.when(early_next)
        def _():
            edge_forward(k).start()

        @pl.when(early_prev)
        def _():
            edge_backward(k).start()

        return 0

    lax.fori_loop(0, WINDOWS, edge_stage, 0)

    def middle_row(k, j):
        rows = rows_of(k, j)
        return row_lift(rows[0::2], rows[1::2], *[nothing] * 4)[1][1]

    def middle_stage(pair, _):
        k = 2 * pair
        a = [middle_row(k, j) for j in range(WIDE)]
        b = [middle_row(k + 1, j) for j in range(WIDE)]
        even, odd = split_pair(a, b, 1, lane_even)
        even, odd = column_lift(even, odd, 2, lane, KAPPA * KAPPA)
        for n, row in enumerate(join_pair(even, odd, 1, lane_even)):
            put_row(k + n, 3, row, first=True)
            start_blocks(k + n, 0)
        return 0

    lax.fori_loop(0, WINDOWS // 2, middle_stage, 0)

    @pl.when(late_next)
    def _():
        pl.semaphore_wait(ready.at[0], 1)

        def forward_stage(k, _):
            edge_forward(k).start()
            return 0

        lax.fori_loop(0, WINDOWS, forward_stage, 0)

    @pl.when(late_prev)
    def _():
        pl.semaphore_wait(ready.at[1], 1)

        def backward_stage(k, _):
            edge_backward(k).start()
            return 0

        lax.fori_loop(0, WINDOWS, backward_stage, 0)

    def wait_prev(k):
        @pl.when(has_prev)
        def _():
            edge_forward(k).wait_recv()

    def wait_next(k):
        @pl.when(has_next)
        def _():
            edge_backward(k).wait_recv()

    def row_1_stage(k):
        row_1 = []
        for j in range(WIDE):
            rows = rows_of(k, j)
            rest = [nothing] * 3
            row_1.append(row_lift(rows[0::2], rows[1::2], from_prev[k, j, 0], *rest)[1][0])
        even, odd = row_1, [turn(v, -1) for v in row_1]
        even, odd = column_lift(even, odd, 2, lane, KAPPA * KAPPA)
        put_row(k, 1, [jnp.where(lane_even, e, turn(o, 1)) for e, o in zip(even, odd)])
        start_blocks(k, 2)

    def rows_5_7_stage(k):
        row_5, row_7 = [], []
        for j in range(WIDE):
            rows = rows_of(k, j)
            edges = (nothing, nothing, from_next[k, j, 0], from_next[k, j, 1])
            odd = row_lift(rows[0::2], rows[1::2], *edges)[1]
            row_5.append(odd[2])
            row_7.append(odd[3])
        even, odd = split_pair(row_5, row_7, 1, lane_even)
        even, odd = column_lift(even, odd, 2, lane, KAPPA * KAPPA)
        row_5, row_7 = join_pair(even, odd, 1, lane_even)
        put_row(k, 5, row_5)
        put_row(k, 7, row_7)
        start_blocks(k, 1)

    def first_stage(k):
        w = window_of(k)
        for j in range(WIDE):
            rows = rows_of(k, j)
            even, _ = row_lift(
                rows[0::2],
                rows[1::2],
                from_prev[k, j, 0],
                from_prev[k, j, 1],
                from_next[k, j, 0],
                from_next[k, j, 1],
            )
            for i in range(4):
                window[i, j] = even[i]

        def split(a, b):
            tiles = [[window[i, j] for j in range(WIDE)] for i in (a, b)]
            return split_pair(*tiles, 1, lane_even)

        within = jnp.logical_or(
            lane < LAST,
            jnp.logical_or(
                jnp.logical_and(lane < LAST + HALO, w < WINDOWS - 1),
                jnp.logical_and(lane >= LAST + HALO, w > 0),
            ),
        )
        low_a, high_a = column_lift(*split(0, 2), 2, lane)
        low_b, high_b = column_lift(*split(1, 3), 2, lane)
        low_a[-1] = jnp.where(within, low_a[-1], 0.0)
        low_b[-1] = jnp.where(within, low_b[-1], 0.0)
        even, odd = split_pair(low_a, low_b, 2, lane_low)
        even, odd = column_lift(even, odd, 4, lane)
        low_a, low_b = join_pair(even, odd, 2, lane_low)
        c0, c2 = join_pair(low_a, high_a, 1, lane_even)
        c1, c3 = join_pair(low_b, high_b, 1, lane_even)
        for j in range(WIDE):
            for i, row in enumerate((c0, c1, c2, c3)):
                hold[k, i, j] = row[j]
            (p, q), (r, s) = row_messages([c0[j], c2[j]], [c1[j], c3[j]])
            to_next2[k, j] = jnp.where(lane_even, p, turn(q, 1))
            to_prev2[k, j] = jnp.where(lane_even, r, turn(s, 1))

        @pl.when(has_next)
        def _():
            edge2_forward(k).start()

        @pl.when(has_prev)
        def _():
            edge2_backward(k).start()

    square = KAPPA * KAPPA
    one = jnp.ones((ROWS, LANES), jnp.float32)
    scale_even = jnp.where(
        lane_even, jnp.where(lane_low, 1.0 / (square * square), 1.0 / square), one
    )
    scale_odd = jnp.where(jnp.logical_and(lane_even, lane_low), 1.0 / square, one)

    def second_stage(k):
        @pl.when(has_prev)
        def _():
            edge2_forward(k).wait_recv()

        @pl.when(has_next)
        def _():
            edge2_backward(k).wait_recv()

        rows = [[None] * WIDE for _ in range(4)]
        for j in range(WIDE):
            c = [hold[k, i, j] for i in range(4)]
            p = from_prev2[k, j]
            r = from_next2[k, j]
            even, odd = row_lift(c[0::2], c[1::2], p, turn(p, -1), r, turn(r, -1))
            for i in range(2):
                rows[2 * i][j] = jnp.where(lane_even, even[i], c[2 * i]) * scale_even
                rows[2 * i + 1][j] = jnp.where(lane_even, odd[i], c[2 * i + 1]) * scale_odd
        for i in range(4):
            put_row(k, 2 * i, rows[i], first=i == 0)
        start_blocks(k, 3)

    @pl.when(row_1_first)
    def _():
        def early_stage(k, _):
            wait_prev(k)
            row_1_stage(k)
            return 0

        lax.fori_loop(0, WINDOWS, early_stage, 0)

    @pl.when(seam_prev)
    def _():
        def early_stage(k, _):
            wait_next(k)
            rows_5_7_stage(k)
            return 0

        lax.fori_loop(0, WINDOWS, early_stage, 0)

    def stages(k, _):
        @pl.when(k < WINDOWS)
        def _():
            @pl.when(jnp.logical_not(row_1_first))
            def _():
                wait_prev(k)

            @pl.when(jnp.logical_not(seam_prev))
            def _():
                wait_next(k)

            first_stage(k)

            @pl.when(jnp.logical_not(row_1_first))
            def _():
                row_1_stage(k)

            @pl.when(jnp.logical_not(seam_prev))
            def _():
                rows_5_7_stage(k)

        @pl.when(k >= 2)
        def _():
            second_stage(k - 2)

        return 0

    lax.fori_loop(0, WINDOWS + 2, stages, 0)

    def spread(source):
        for row in range(ROWS):
            start = (source * ROWS + row) * SPAN * ROWS
            for j in range(FULL):
                levels[pl.ds(pl.multiple_of(start + j * ROWS, ROWS), ROWS), :] = recv[
                    source, pl.ds(ROW_AT[row] + j * ROWS, ROWS), :
                ]
            tail = recv[source, pl.ds(ODD_TAILS if row % 2 else EVEN_TAILS, ROWS), :]
            levels[pl.ds(pl.multiple_of(start + FULL * ROWS, ROWS), ROWS), :] = turn(
                tail, -TAIL * TAIL_AT[row]
            )

    low_taps, high_taps = tap_values()
    cutoffs = [cutoff_pattern(pointer_ref, part) for part in range(2)]

    def level_tile(source, level, j):
        start = source * ROWS * SPAN * ROWS + j * ROWS + level
        return levels[pl.ds(start, ROWS, stride=SPAN * ROWS), :]

    def put_pair(source, i, j, taken):
        for part, taps in enumerate((low_taps, high_taps)):
            value = taps[0] * taken[0]
            for tap in range(1, 4):
                value = value + taps[tap] * taken[tap]
            cutoff = cutoffs[part]
            value = value - jnp.minimum(jnp.maximum(value, -cutoff), cutoff)
            row = part * PARTS * ROWS // 2 + source * (ROWS // 2) + i
            if j == FULL:
                out_ref[row, :, pl.ds(FULL * LANES, TAIL)] = value[:, :TAIL]
            else:
                out_ref[row, :, pl.ds(j * LANES, LANES)] = value

    def store(source, part, last):
        start = part * PARTS * ROWS // 2 + source * (ROWS // 2)
        some = pl.ds(start + 3, 1) if last else pl.ds(start, 3)
        return pltpu.make_async_copy(
            out_ref.at[some], out_hbm.at[some], store_sem.at[2 * part + last, source]
        )

    def within_source(source):
        spread(source)
        for j in range(SPAN):
            taken = [level_tile(source, level, j) for level in range(ROWS)]
            for i in range(ROWS // 2 - 1):
                put_pair(source, i, j, taken[2 * i : 2 * i + 4])
        for part in range(2):
            store(source, part, 0).start()

    def arrived(n, _):
        step = (n + 1) // 2
        source = 2 * lax.rem(place + WINDOWS - step, WINDOWS) + lax.rem(half + n, 2)

        @pl.when(n == 0)
        def _():
            for piece in range(len(PIECES)):
                own_copy(piece).wait()

        @pl.when(n > 0)
        def _():
            for piece in range(len(PIECES)):
                from_source(source, piece).wait_recv()

        within_source(source)
        return 0

    lax.fori_loop(0, PARTS, arrived, 0)

    def across_sources(source, _):
        after = lax.rem(source + 1, PARTS)
        for j in range(SPAN):
            taken = [level_tile(source, level, j) for level in (ROWS - 2, ROWS - 1)]
            taken += [level_tile(after, level, j) for level in range(2)]
            put_pair(source, ROWS // 2 - 1, j, taken)
        for part in range(2):
            store(source, part, 1).start()
        return 0

    lax.fori_loop(0, PARTS, across_sources, 0)

    def sent(k, _):
        @pl.when(has_next)
        def _():
            edge_forward(k).wait_send()
            edge2_forward(k).wait_send()

        @pl.when(has_prev)
        def _():
            edge_backward(k).wait_send()
            edge2_backward(k).wait_send()

        for b in range(2):

            @pl.when(jnp.logical_not(jnp.logical_and(k == WINDOWS - 1, half == b)))
            def _():
                for piece in range(len(PIECES)):
                    block_copy(k, b, piece).wait_send()

        return 0

    lax.fori_loop(0, WINDOWS, sent, 0)

    def stored(source, _):
        for part in range(2):
            for last in range(2):
                store(source, part, last).wait()
        return 0

    lax.fori_loop(0, PARTS, stored, 0)


def local(tiles_count, thermal_deviation, terrain_flag, frequency_share_limit_pointer):
    tile = (ROWS, LANES)
    vmem = lambda *shape: pltpu.VMEM(shape, jnp.float32)
    dma = pltpu.SemaphoreType.DMA
    return pl.pallas_call(
        functools.partial(kernel, tiles_count),
        out_shape=jax.ShapeDtypeStruct((PARTS * ROWS, ROWS, BLOCK), jnp.float32),
        in_specs=[
            pl.BlockSpec(memory_space=pltpu.HBM),
            pl.BlockSpec(memory_space=pltpu.HBM),
            pl.BlockSpec(memory_space=pltpu.SMEM),
        ],
        out_specs=pl.BlockSpec(memory_space=pltpu.HBM),
        scratch_shapes=[
            vmem(PARTS * ROWS, ROWS, BLOCK),
            vmem(ROWS, ROWS, WIDTH),
            pltpu.VMEM((ROWS, WIDTH), jnp.int32),
            vmem(PADDED * GROUP, LANES),
            vmem(WINDOWS * WIDE * GROUP, LANES),
            vmem(WINDOWS, WIDE, 2, *tile),
            vmem(WINDOWS, WIDE, 2, *tile),
            vmem(WINDOWS, WIDE, 2, *tile),
            vmem(WINDOWS, WIDE, 2, *tile),
            vmem(4, WIDE, *tile),
            vmem(WINDOWS, 4, WIDE, *tile),
            vmem(WINDOWS, WIDE, *tile),
            vmem(WINDOWS, WIDE, *tile),
            vmem(WINDOWS, WIDE, *tile),
            vmem(WINDOWS, WIDE, *tile),
            vmem(PARTS, MESSAGE, LANES),
            vmem(PARTS, MESSAGE, LANES),
            vmem(PARTS * ROWS * SPAN * ROWS, LANES),
            dma((ROWS + 1,)),
            dma((2, WINDOWS)),
            dma((2, WINDOWS)),
            dma((2, WINDOWS)),
            dma((2, WINDOWS)),
            dma((len(PIECES), PARTS)),
            dma((len(PIECES), PARTS)),
            dma((len(PIECES),)),
            dma((4, PARTS)),
            pltpu.SemaphoreType.REGULAR((2,)),
        ],
        compiler_params=pltpu.CompilerParams(
            collective_id=0, has_side_effects=True, vmem_limit_bytes=60 * 1024 * 1024
        ),
    )(thermal_deviation, terrain_flag, frequency_share_limit_pointer)


def solution(mesh):
    placed = (P("lev", "tile", None), P("tile", None), P())
    return jax.shard_map(
        functools.partial(local, mesh.shape["tile"]),
        mesh=mesh,
        in_specs=placed,
        out_specs=P(None, "tile", "lev"),
        check_vma=False,
    )
```

```python
import functools
import math

import jax
import jax.numpy as jnp
import numpy as np
from jax import lax
from jax.experimental import pallas as pl
from jax.experimental.pallas import tpu as pltpu
from jax.sharding import PartitionSpec as P

ALPHA = -1.586134342
BETA = -0.05298011854
GAMMA = 0.8829110762
DELTA = 0.4435068522
KAPPA = 1.149604398

LANES = 128
ROWS = 8
WIDTH = 4320
PARTS = 8
BLOCK = WIDTH // PARTS
FULL = BLOCK // LANES
TAIL = BLOCK - FULL * LANES
SPAN = FULL + 1
WINDOWS = 4
WIDE = 9
LAST = 2 * BLOCK - (WIDE - 1) * LANES
HALO = (LANES - LAST) // 2
PADDED = 36
GROUP = ROWS * ROWS
ROW_LINES = FULL * ROWS
SLOTS = (3, 5, 7, 1, 0, 2, 4, 6)
ROW_AT = {row: i * ROW_LINES for i, row in enumerate(SLOTS)}
ODD_TAILS = ROWS * ROW_LINES
EVEN_TAILS = ODD_TAILS + ROWS
MESSAGE = EVEN_TAILS + ROWS
PIECES = (
    (0, ROW_LINES),
    (ROW_LINES, 2 * ROW_LINES),
    (3 * ROW_LINES, ROW_LINES),
    (4 * ROW_LINES, MESSAGE - 4 * ROW_LINES),
)
TAIL_AT = {row: row // 2 for row in range(ROWS)}
CHAIN = 8
MESH = pl.DeviceIdType.MESH


def impulse_responses():
    low, high = [], []
    for distance in range(5):
        for centre, taps in ((16, low), (17, high)):
            signal = np.zeros(34)
            signal[centre + distance] = 1.0
            even, odd = signal[0::2].copy(), signal[1::2].copy()
            odd[:-1] += ALPHA * (even[:-1] + even[1:])
            even[1:] += BETA * (odd[:-1] + odd[1:])
            odd[:-1] += GAMMA * (even[:-1] + even[1:])
            even[1:] += DELTA * (odd[:-1] + odd[1:])
            taps.append(float(even[8] if centre == 16 else odd[8]))
    return low, high[:4]


LOW, HIGH = impulse_responses()


def row_messages(even, odd):
    first = odd[0] + ALPHA * (even[0] + even[1])
    before = odd[-2] + ALPHA * (even[-2] + even[-1])
    p = odd[-1] + ALPHA * even[-1]
    q = p + GAMMA * (even[-1] + BETA * (before + p))
    return (p, q), (even[0], first)


def row_lift(even, odd, p, q, r, s):
    n = len(even)
    odd_one = [p + ALPHA * even[0]]
    odd_one += [odd[j] + ALPHA * (even[j] + (even[j + 1] if j + 1 < n else r)) for j in range(n)]
    even_two = [even[j] + BETA * (odd_one[j] + odd_one[j + 1]) for j in range(n)]
    even_two.append(r + BETA * (odd_one[n] + s))
    odd_three = [q + (ALPHA * (1.0 + GAMMA * BETA)) * even[0] + GAMMA * even_two[0]]
    odd_three += [odd_one[j + 1] + GAMMA * (even_two[j] + even_two[j + 1]) for j in range(n)]
    even_four = [even_two[j] + DELTA * (odd_three[j] + odd_three[j + 1]) for j in range(n)]
    return even_four, odd_three[1:]


def turn(value, amount):
    return pltpu.roll(value, amount % LANES, axis=1)


def column_lift(even, odd, step, lane, high_scale=1.0):
    n = len(even)

    def moved(tiles, distance):
        lanes = distance * step
        rolled = [turn(v, -lanes) for v in tiles]
        if distance > 0:
            return [jnp.where(lane >= LANES - lanes, rolled[(j + 1) % n], rolled[j]) for j in range(n)]
        return [jnp.where(lane < -lanes, rolled[j - 1], rolled[j]) for j in range(n)]

    even_at = {d: moved(even, d) for d in (-2, -1, 1, 2)}
    odd_at = {d: moved(odd, d) for d in (-2, -1, 1)}
    high_taps = [high_scale * tap for tap in HIGH]
    low, high = [], []
    for j in range(n):
        low.append(
            LOW[0] * even[j]
            + LOW[1] * (odd_at[-1][j] + odd[j])
            + LOW[2] * (even_at[-1][j] + even_at[1][j])
            + LOW[3] * (odd_at[-2][j] + odd_at[1][j])
            + LOW[4] * (even_at[-2][j] + even_at[2][j])
        )
        high.append(
            high_taps[0] * odd[j]
            + high_taps[1] * (even[j] + even_at[1][j])
            + high_taps[2] * (odd_at[-1][j] + odd_at[1][j])
            + high_taps[3] * (even_at[-1][j] + even_at[2][j])
        )
    return low, high


def split_pair(a, b, step, keep):
    even = [jnp.where(keep, u, turn(v, step)) for u, v in zip(a, b)]
    odd = [jnp.where(keep, turn(u, -step), v) for u, v in zip(a, b)]
    return even, odd


def join_pair(even, odd, step, keep):
    a = [jnp.where(keep, e, turn(o, step)) for e, o in zip(even, odd)]
    b = [jnp.where(keep, turn(e, -step), o) for e, o in zip(even, odd)]
    return a, b


def tap_values():
    root = math.sqrt(3.0)
    scale = 4.0 * math.sqrt(2.0)
    low = [(1.0 + root) / scale, (3.0 + root) / scale, (3.0 - root) / scale, (1.0 - root) / scale]
    return low, [low[3], -low[2], low[1], -low[0]]


def cutoff_pattern(pointer_ref, half):
    row = lax.broadcasted_iota(jnp.int32, (ROWS, LANES), 0)
    col = lax.broadcasted_iota(jnp.int32, (ROWS, LANES), 1)
    fine = 3 + 2 * (row % 2) + col % 2
    coarse = 2 * (row // 2 % 2) + col // 2 % 2
    band = jnp.where(row % 2 + col % 2 > 0, fine, coarse)
    power = jnp.zeros((ROWS, LANES), jnp.int32)
    for number in range(7):
        power = jnp.where(band == number, pointer_ref[7 * half + number], power)
    cutoff = jnp.full((ROWS, LANES), 0.05, jnp.float32)
    for bit in range(4):
        factor = 1.25 ** (2**bit)
        cutoff = jnp.where((power // 2**bit) % 2 == 1, cutoff * factor, cutoff)
    return cutoff


def kernel(
    tiles_count,
    x_hbm,
    flag_hbm,
    pointer_hbm,
    out_ref,
    pointer_ref,
    x_ref,
    flag_ref,
    field,
    aligned,
    to_next,
    to_prev,
    from_prev,
    from_next,
    window,
    hold,
    to_next2,
    to_prev2,
    from_prev2,
    from_next2,
    send,
    recv,
    levels,
    load_sem,
    edge_send,
    edge_recv,
    edge2_send,
    edge2_recv,
    block_send,
    block_recv,
    own_sem,
    ready,
):
    me = lax.axis_index("lev")
    row_block = lax.axis_index("tile")
    place, half = me // 2, lax.rem(me, 2)
    has_prev = row_block > 0
    has_next = row_block < tiles_count - 1
    seam_prev = lax.rem(row_block, CHAIN) == 0
    late_prev = jnp.logical_and(has_prev, seam_prev)
    late_next = jnp.logical_and(has_next, lax.rem(row_block, CHAIN) == CHAIN // 2 - 1)
    seen_by_prev = jnp.logical_and(has_prev, lax.rem(row_block, CHAIN) == CHAIN // 2)
    seen_by_next = jnp.logical_and(has_next, lax.rem(row_block, CHAIN) == CHAIN - 1)
    early_prev = jnp.logical_and(has_prev, jnp.logical_not(late_prev))
    early_next = jnp.logical_and(has_next, jnp.logical_not(late_next))
    row_1_first = lax.rem(row_block, CHAIN) == 1
    lane = lax.broadcasted_iota(jnp.int32, (ROWS, LANES), 1)
    lane_even = lane % 2 == 0
    lane_low = lane % 4 < 2
    nothing = jnp.zeros((ROWS, LANES), jnp.float32)

    barrier = pltpu.get_barrier_semaphore()
    for step in range(1, PARTS):
        pl.semaphore_signal(
            barrier,
            inc=1,
            device_id={"lev": lax.rem(me + step, PARTS)},
            device_id_type=MESH,
        )

    @pl.when(jnp.logical_and(has_prev, jnp.logical_not(seen_by_prev)))
    def _():
        pl.semaphore_signal(
            barrier, inc=1, device_id={"tile": row_block - 1}, device_id_type=MESH
        )

    @pl.when(jnp.logical_and(has_next, jnp.logical_not(seen_by_next)))
    def _():
        pl.semaphore_signal(
            barrier, inc=1, device_id={"tile": row_block + 1}, device_id_type=MESH
        )

    loads = [
        pltpu.make_async_copy(x_hbm.at[level], x_ref.at[level], load_sem.at[level])
        for level in range(ROWS)
    ]
    loads.append(pltpu.make_async_copy(flag_hbm, flag_ref, load_sem.at[ROWS]))
    loads.append(pltpu.make_async_copy(pointer_hbm, pointer_ref, load_sem.at[ROWS + 1]))
    for load in loads:
        load.start()

    def clear(edge, edge2):
        def clear_window(k, _):
            for j in range(WIDE):
                edge[k, j, 0] = nothing
                edge[k, j, 1] = nothing
                edge2[k, j] = nothing
            return 0

        lax.fori_loop(0, WINDOWS, clear_window, 0)

    @pl.when(jnp.logical_not(has_prev))
    def _():
        clear(from_prev, from_prev2)

    @pl.when(jnp.logical_not(has_next))
    def _():
        clear(from_next, from_next2)

    field[pl.ds(0, GROUP), :] = jnp.zeros((GROUP, LANES), jnp.float32)
    field[pl.ds((PADDED - 2) * GROUP, 2 * GROUP), :] = jnp.zeros((2 * GROUP, LANES), jnp.float32)
    pl.semaphore_wait(
        barrier, PARTS - 1 + jnp.where(early_prev, 1, 0) + jnp.where(early_next, 1, 0)
    )

    @pl.when(seen_by_prev)
    def _():
        pl.semaphore_signal(
            ready.at[0], inc=1, device_id={"tile": row_block - 1}, device_id_type=MESH
        )

    @pl.when(seen_by_next)
    def _():
        pl.semaphore_signal(
            ready.at[1], inc=1, device_id={"tile": row_block + 1}, device_id_type=MESH
        )

    for load in loads:
        load.wait()

    whole = WIDTH // LANES
    rest = WIDTH - whole * LANES

    def load_tile(tile, _):
        columns = pl.ds(pl.multiple_of(tile * LANES, LANES), LANES)
        water = (1 - flag_ref[:, columns]).astype(jnp.float32)
        for level in range(ROWS):
            start = pl.multiple_of((tile + 1) * GROUP + level * ROWS, ROWS)
            field[pl.ds(start, ROWS), :] = x_ref[level, :, columns] * water
        return 0

    lax.fori_loop(0, whole, load_tile, 0)
    water = (1 - flag_ref[:, pl.ds(whole * LANES, rest)]).astype(jnp.float32)
    for level in range(ROWS):
        start = (whole + 1) * GROUP + level * ROWS
        field[pl.ds(start, ROWS), pl.ds(0, rest)] = (
            x_ref[level, :, pl.ds(whole * LANES, rest)] * water
        )

    def window_of(k):
        return lax.rem(place + 1 + k, WINDOWS)

    def edge_forward(k):
        return pltpu.make_async_remote_copy(
            src_ref=to_next.at[k],
            dst_ref=from_prev.at[k],
            send_sem=edge_send.at[0, k],
            recv_sem=edge_recv.at[0, k],
            device_id={"tile": row_block + 1},
            device_id_type=MESH,
        )

    def edge_backward(k):
        return pltpu.make_async_remote_copy(
            src_ref=to_prev.at[k],
            dst_ref=from_next.at[k],
            send_sem=edge_send.at[1, k],
            recv_sem=edge_recv.at[1, k],
            device_id={"tile": row_block - 1},
            device_id_type=MESH,
        )

    def edge2_forward(k):
        return pltpu.make_async_remote_copy(
            src_ref=to_next2.at[k],
            dst_ref=from_prev2.at[k],
            send_sem=edge2_send.at[0, k],
            recv_sem=edge2_recv.at[0, k],
            device_id={"tile": row_block + 1},
            device_id_type=MESH,
        )

    def edge2_backward(k):
        return pltpu.make_async_remote_copy(
            src_ref=to_prev2.at[k],
            dst_ref=from_next2.at[k],
            send_sem=edge2_send.at[1, k],
            recv_sem=edge2_recv.at[1, k],
            device_id={"tile": row_block - 1},
            device_id_type=MESH,
        )

    def block_copy(k, b, piece):
        lines = pl.ds(*PIECES[piece])
        return pltpu.make_async_remote_copy(
            src_ref=send.at[2 * k + b, lines],
            dst_ref=recv.at[me, lines],
            send_sem=block_send.at[piece, 2 * k + b],
            recv_sem=block_recv.at[piece, me],
            device_id={"lev": 2 * window_of(k) + b},
            device_id_type=MESH,
        )

    def from_source(source, piece):
        lines = pl.ds(*PIECES[piece])
        return pltpu.make_async_remote_copy(
            src_ref=send.at[0, lines],
            dst_ref=recv.at[source, lines],
            send_sem=block_send.at[piece, 0],
            recv_sem=block_recv.at[piece, source],
            device_id={"lev": source},
            device_id_type=MESH,
        )

    def own_copy(piece):
        lines = pl.ds(*PIECES[piece])
        return pltpu.make_async_copy(
            send.at[2 * (WINDOWS - 1) + half, lines], recv.at[me, lines], own_sem.at[piece]
        )

    def start_blocks(k, piece):
        for b in range(2):
            is_own = jnp.logical_and(k == WINDOWS - 1, half == b)

            @pl.when(jnp.logical_not(is_own))
            def _():
                block_copy(k, b, piece).start()

            @pl.when(is_own)
            def _():
                own_copy(piece).start()

    def put_row(k, row, tiles, first=False):
        at = ROW_AT[row]
        for j in range(FULL):
            send[2 * k, pl.ds(at + j * ROWS, ROWS), :] = tiles[j]
        rolled = [turn(tiles[j], -TAIL) for j in range(FULL, WIDE)]
        for j in range(FULL):
            send[2 * k + 1, pl.ds(at + j * ROWS, ROWS), :] = jnp.where(
                lane < LANES - TAIL, rolled[j], rolled[j + 1]
            )
        start = TAIL * TAIL_AT[row]
        lines = pl.ds(ODD_TAILS if row % 2 else EVEN_TAILS, ROWS)
        for b, tail in enumerate((tiles[FULL], rolled[FULL])):
            tail = turn(tail, start)
            if not first:
                mine = jnp.logical_and(lane >= start, lane < start + TAIL)
                tail = jnp.where(mine, tail, send[2 * k + b, lines, :])
            send[2 * k + b, lines, :] = tail

    def rows_of(k, j):
        start = (k * WIDE + j) * GROUP
        return [aligned[pl.ds(start + row, ROWS, stride=ROWS), :] for row in range(ROWS)]

    def edge_stage(k, _):
        w = window_of(k)
        first = (w * 2 * BLOCK) // LANES
        shift = w * 2 * BLOCK - first * LANES
        back = lax.rem(LANES - shift, LANES)
        inside = lane < LANES - shift
        halo, before = None, None
        for i in range(WIDE + 2):
            tile = [
                pltpu.roll(
                    field[pl.ds(pl.multiple_of((first + i) * GROUP + level * ROWS, ROWS), ROWS), :],
                    back,
                    axis=1,
                )
                for level in range(ROWS)
            ]
            if i > 0:
                moved = [jnp.where(inside, u, v) for u, v in zip(before, tile)]
                if i == 1:
                    halo = moved
                else:
                    if i == WIDE + 1:
                        moved = [
                            jnp.where(lane < LAST + HALO, u, v) for u, v in zip(moved, halo)
                        ]
                    for level in range(ROWS):
                        start = (k * WIDE + i - 2) * GROUP + level * ROWS
                        aligned[pl.ds(pl.multiple_of(start, ROWS), ROWS), :] = moved[level]
            before = tile
        for j in range(WIDE):
            rows = rows_of(k, j)
            forward, backward = row_messages(rows[0::2], rows[1::2])
            for i in range(2):
                to_next[k, j, i] = forward[i]
                to_prev[k, j, i] = backward[i]

        @pl.when(early_next)
        def _():
            edge_forward(k).start()

        @pl.when(early_prev)
        def _():
            edge_backward(k).start()

        return 0

    lax.fori_loop(0, WINDOWS, edge_stage, 0)

    def middle_row(k, j):
        rows = rows_of(k, j)
        return row_lift(rows[0::2], rows[1::2], *[nothing] * 4)[1][1]

    def middle_stage(pair, _):
        k = 2 * pair
        a = [middle_row(k, j) for j in range(WIDE)]
        b = [middle_row(k + 1, j) for j in range(WIDE)]
        even, odd = split_pair(a, b, 1, lane_even)
        even, odd = column_lift(even, odd, 2, lane, KAPPA * KAPPA)
        for n, row in enumerate(join_pair(even, odd, 1, lane_even)):
            put_row(k + n, 3, row, first=True)
            start_blocks(k + n, 0)
        return 0

    lax.fori_loop(0, WINDOWS // 2, middle_stage, 0)

    @pl.when(late_next)
    def _():
        pl.semaphore_wait(ready.at[0], 1)

        def forward_stage(k, _):
            edge_forward(k).start()
            return 0

        lax.fori_loop(0, WINDOWS, forward_stage, 0)

    def wait_prev(k):
        @pl.when(has_prev)
        def _():
            edge_forward(k).wait_recv()

    def wait_next(k):
        @pl.when(has_next)
        def _():
            edge_backward(k).wait_recv()

    def row_1_stage(k):
        row_1 = []
        for j in range(WIDE):
            rows = rows_of(k, j)
            rest = [nothing] * 3
            row_1.append(row_lift(rows[0::2], rows[1::2], from_prev[k, j, 0], *rest)[1][0])
        even, odd = row_1, [turn(v, -1) for v in row_1]
        even, odd = column_lift(even, odd, 2, lane, KAPPA * KAPPA)
        put_row(k, 1, [jnp.where(lane_even, e, turn(o, 1)) for e, o in zip(even, odd)])
        start_blocks(k, 2)

    def rows_5_7_stage(k):
        row_5, row_7 = [], []
        for j in range(WIDE):
            rows = rows_of(k, j)
            edges = (nothing, nothing, from_next[k, j, 0], from_next[k, j, 1])
            odd = row_lift(rows[0::2], rows[1::2], *edges)[1]
            row_5.append(odd[2])
            row_7.append(odd[3])
        even, odd = split_pair(row_5, row_7, 1, lane_even)
        even, odd = column_lift(even, odd, 2, lane, KAPPA * KAPPA)
        row_5, row_7 = join_pair(even, odd, 1, lane_even)
        put_row(k, 5, row_5)
        put_row(k, 7, row_7)
        start_blocks(k, 1)

    def first_stage(k):
        w = window_of(k)
        for j in range(WIDE):
            rows = rows_of(k, j)
            even, _ = row_lift(
                rows[0::2],
                rows[1::2],
                from_prev[k, j, 0],
                from_prev[k, j, 1],
                from_next[k, j, 0],
                from_next[k, j, 1],
            )
            for i in range(4):
                window[i, j] = even[i]

        def split(a, b):
            tiles = [[window[i, j] for j in range(WIDE)] for i in (a, b)]
            return split_pair(*tiles, 1, lane_even)

        within = jnp.logical_or(
            lane < LAST,
            jnp.logical_or(
                jnp.logical_and(lane < LAST + HALO, w < WINDOWS - 1),
                jnp.logical_and(lane >= LAST + HALO, w > 0),
            ),
        )
        low_a, high_a = column_lift(*split(0, 2), 2, lane)
        low_b, high_b = column_lift(*split(1, 3), 2, lane)
        low_a[-1] = jnp.where(within, low_a[-1], 0.0)
        low_b[-1] = jnp.where(within, low_b[-1], 0.0)
        even, odd = split_pair(low_a, low_b, 2, lane_low)
        even, odd = column_lift(even, odd, 4, lane)
        low_a, low_b = join_pair(even, odd, 2, lane_low)
        c0, c2 = join_pair(low_a, high_a, 1, lane_even)
        c1, c3 = join_pair(low_b, high_b, 1, lane_even)
        for j in range(WIDE):
            for i, row in enumerate((c0, c1, c2, c3)):
                hold[k, i, j] = row[j]
            (p, q), (r, s) = row_messages([c0[j], c2[j]], [c1[j], c3[j]])
            to_next2[k, j] = jnp.where(lane_even, p, turn(q, 1))
            to_prev2[k, j] = jnp.where(lane_even, r, turn(s, 1))

        @pl.when(has_next)
        def _():
            edge2_forward(k).start()

        @pl.when(has_prev)
        def _():
            edge2_backward(k).start()

    square = KAPPA * KAPPA
    one = jnp.ones((ROWS, LANES), jnp.float32)
    scale_even = jnp.where(
        lane_even, jnp.where(lane_low, 1.0 / (square * square), 1.0 / square), one
    )
    scale_odd = jnp.where(jnp.logical_and(lane_even, lane_low), 1.0 / square, one)

    def second_stage(k):
        @pl.when(has_prev)
        def _():
            edge2_forward(k).wait_recv()

        @pl.when(has_next)
        def _():
            edge2_backward(k).wait_recv()

        rows = [[None] * WIDE for _ in range(4)]
        for j in range(WIDE):
            c = [hold[k, i, j] for i in range(4)]
            p = from_prev2[k, j]
            r = from_next2[k, j]
            even, odd = row_lift(c[0::2], c[1::2], p, turn(p, -1), r, turn(r, -1))
            for i in range(2):
                rows[2 * i][j] = jnp.where(lane_even, even[i], c[2 * i]) * scale_even
                rows[2 * i + 1][j] = jnp.where(lane_even, odd[i], c[2 * i + 1]) * scale_odd
        for i in range(4):
            put_row(k, 2 * i, rows[i], first=i == 0)
        start_blocks(k, 3)

    @pl.when(row_1_first)
    def _():
        def early_stage(k, _):
            wait_prev(k)
            row_1_stage(k)
            return 0

        lax.fori_loop(0, WINDOWS, early_stage, 0)

    @pl.when(seam_prev)
    def _():
        def early_stage(k, _):
            wait_next(k)
            rows_5_7_stage(k)
            return 0

        lax.fori_loop(0, WINDOWS, early_stage, 0)

    @pl.when(late_prev)
    def _():
        pl.semaphore_wait(ready.at[1], 1)

        def backward_stage(k, _):
            edge_backward(k).start()
            return 0

        lax.fori_loop(0, WINDOWS, backward_stage, 0)

    def stages(k, _):
        @pl.when(k < WINDOWS)
        def _():
            @pl.when(jnp.logical_not(row_1_first))
            def _():
                wait_prev(k)

            @pl.when(jnp.logical_not(seam_prev))
            def _():
                wait_next(k)

            first_stage(k)

            @pl.when(jnp.logical_not(row_1_first))
            def _():
                row_1_stage(k)

            @pl.when(jnp.logical_not(seam_prev))
            def _():
                rows_5_7_stage(k)

        @pl.when(k >= 2)
        def _():
            second_stage(k - 2)

        return 0

    lax.fori_loop(0, WINDOWS + 2, stages, 0)

    def spread(source):
        for row in range(ROWS):
            start = (source * ROWS + row) * SPAN * ROWS
            for j in range(FULL):
                levels[pl.ds(pl.multiple_of(start + j * ROWS, ROWS), ROWS), :] = recv[
                    source, pl.ds(ROW_AT[row] + j * ROWS, ROWS), :
                ]
            tail = recv[source, pl.ds(ODD_TAILS if row % 2 else EVEN_TAILS, ROWS), :]
            levels[pl.ds(pl.multiple_of(start + FULL * ROWS, ROWS), ROWS), :] = turn(
                tail, -TAIL * TAIL_AT[row]
            )

    low_taps, high_taps = tap_values()
    cutoffs = [cutoff_pattern(pointer_ref, part) for part in range(2)]

    def level_tile(source, level, j):
        start = source * ROWS * SPAN * ROWS + j * ROWS + level
        return levels[pl.ds(start, ROWS, stride=SPAN * ROWS), :]

    def put_pair(source, i, j, taken):
        for part, taps in enumerate((low_taps, high_taps)):
            value = taps[0] * taken[0]
            for tap in range(1, 4):
                value = value + taps[tap] * taken[tap]
            cutoff = cutoffs[part]
            value = value - jnp.minimum(jnp.maximum(value, -cutoff), cutoff)
            row = part * PARTS * ROWS // 2 + source * (ROWS // 2) + i
            if j == FULL:
                out_ref[row, :, pl.ds(FULL * LANES, TAIL)] = value[:, :TAIL]
            else:
                out_ref[row, :, pl.ds(j * LANES, LANES)] = value

    def within_source(source):
        spread(source)
        for j in range(SPAN):
            taken = [level_tile(source, level, j) for level in range(ROWS)]
            for i in range(ROWS // 2 - 1):
                put_pair(source, i, j, taken[2 * i : 2 * i + 4])

    def arrived(n, _):
        step = (n + 1) // 2
        source = 2 * lax.rem(place + WINDOWS - step, WINDOWS) + lax.rem(half + n, 2)

        @pl.when(n == 0)
        def _():
            for piece in range(len(PIECES)):
                own_copy(piece).wait()

        @pl.when(n > 0)
        def _():
            for piece in range(len(PIECES)):
                from_source(source, piece).wait_recv()

        within_source(source)
        return 0

    lax.fori_loop(0, PARTS, arrived, 0)

    def across_sources(source, _):
        after = lax.rem(source + 1, PARTS)
        for j in range(SPAN):
            taken = [level_tile(source, level, j) for level in (ROWS - 2, ROWS - 1)]
            taken += [level_tile(after, level, j) for level in range(2)]
            put_pair(source, ROWS // 2 - 1, j, taken)
        return 0

    lax.fori_loop(0, PARTS, across_sources, 0)

    def sent(k, _):
        @pl.when(has_next)
        def _():
            edge_forward(k).wait_send()
            edge2_forward(k).wait_send()

        @pl.when(has_prev)
        def _():
            edge_backward(k).wait_send()
            edge2_backward(k).wait_send()

        for b in range(2):

            @pl.when(jnp.logical_not(jnp.logical_and(k == WINDOWS - 1, half == b)))
            def _():
                for piece in range(len(PIECES)):
                    block_copy(k, b, piece).wait_send()

        return 0

    lax.fori_loop(0, WINDOWS, sent, 0)


def local(tiles_count, thermal_deviation, terrain_flag, frequency_share_limit_pointer):
    tile = (ROWS, LANES)
    vmem = lambda *shape: pltpu.VMEM(shape, jnp.float32)
    dma = pltpu.SemaphoreType.DMA
    return pl.pallas_call(
        functools.partial(kernel, tiles_count),
        out_shape=pltpu.VMEM((PARTS * ROWS, ROWS, BLOCK), jnp.float32),
        in_specs=[
            pl.BlockSpec(memory_space=pltpu.HBM),
            pl.BlockSpec(memory_space=pltpu.HBM),
            pl.BlockSpec(memory_space=pltpu.HBM),
        ],
        out_specs=pl.BlockSpec(memory_space=pltpu.VMEM),
        scratch_shapes=[
            pltpu.SMEM((14,), jnp.int32),
            vmem(ROWS, ROWS, WIDTH),
            pltpu.VMEM((ROWS, WIDTH), jnp.int32),
            vmem(PADDED * GROUP, LANES),
            vmem(WINDOWS * WIDE * GROUP, LANES),
            vmem(WINDOWS, WIDE, 2, *tile),
            vmem(WINDOWS, WIDE, 2, *tile),
            vmem(WINDOWS, WIDE, 2, *tile),
            vmem(WINDOWS, WIDE, 2, *tile),
            vmem(4, WIDE, *tile),
            vmem(WINDOWS, 4, WIDE, *tile),
            vmem(WINDOWS, WIDE, *tile),
            vmem(WINDOWS, WIDE, *tile),
            vmem(WINDOWS, WIDE, *tile),
            vmem(WINDOWS, WIDE, *tile),
            vmem(PARTS, MESSAGE, LANES),
            vmem(PARTS, MESSAGE, LANES),
            vmem(PARTS * ROWS * SPAN * ROWS, LANES),
            dma((ROWS + 2,)),
            dma((2, WINDOWS)),
            dma((2, WINDOWS)),
            dma((2, WINDOWS)),
            dma((2, WINDOWS)),
            dma((len(PIECES), PARTS)),
            dma((len(PIECES), PARTS)),
            dma((len(PIECES),)),
            pltpu.SemaphoreType.REGULAR((2,)),
        ],
        compiler_params=pltpu.CompilerParams(
            collective_id=0, has_side_effects=True, vmem_limit_bytes=40 * 1024 * 1024
        ),
    )(
        pltpu.with_memory_space_constraint(thermal_deviation, pltpu.HBM),
        pltpu.with_memory_space_constraint(terrain_flag, pltpu.HBM),
        pltpu.with_memory_space_constraint(frequency_share_limit_pointer, pltpu.HBM),
    )


def solution(mesh):
    placed = (P("lev", "tile", None), P("tile", None), P())
    return jax.shard_map(
        functools.partial(local, mesh.shape["tile"]),
        mesh=mesh,
        in_specs=placed,
        out_specs=P(None, "tile", "lev"),
        check_vma=False,
    )
```

```python
import functools
import math

import jax
import jax.numpy as jnp
import numpy as np
from jax import lax
from jax.experimental import pallas as pl
from jax.experimental.pallas import tpu as pltpu
from jax.sharding import PartitionSpec as P

ALPHA = -1.586134342
BETA = -0.05298011854
GAMMA = 0.8829110762
DELTA = 0.4435068522
KAPPA = 1.149604398

LANES = 128
ROWS = 8
WIDTH = 4320
PARTS = 8
BLOCK = WIDTH // PARTS
FULL = BLOCK // LANES
TAIL = BLOCK - FULL * LANES
SPAN = FULL + 1
WINDOWS = 4
WIDE = 9
LAST = 2 * BLOCK - (WIDE - 1) * LANES
HALO = (LANES - LAST) // 2
PADDED = 36
GROUP = ROWS * ROWS
ROW_LINES = FULL * ROWS
SLOTS = (3, 5, 7, 1, 0, 2, 4, 6)
ROW_AT = {row: i * ROW_LINES for i, row in enumerate(SLOTS)}
ODD_TAILS = ROWS * ROW_LINES
EVEN_TAILS = ODD_TAILS + ROWS
MESSAGE = EVEN_TAILS + ROWS
PIECES = (
    (0, ROW_LINES),
    (ROW_LINES, 2 * ROW_LINES),
    (3 * ROW_LINES, ROW_LINES),
    (4 * ROW_LINES, MESSAGE - 4 * ROW_LINES),
)
TAIL_AT = {row: row // 2 for row in range(ROWS)}
CHAIN = 8
MESH = pl.DeviceIdType.MESH


def impulse_responses():
    low, high = [], []
    for distance in range(5):
        for centre, taps in ((16, low), (17, high)):
            signal = np.zeros(34)
            signal[centre + distance] = 1.0
            even, odd = signal[0::2].copy(), signal[1::2].copy()
            odd[:-1] += ALPHA * (even[:-1] + even[1:])
            even[1:] += BETA * (odd[:-1] + odd[1:])
            odd[:-1] += GAMMA * (even[:-1] + even[1:])
            even[1:] += DELTA * (odd[:-1] + odd[1:])
            taps.append(float(even[8] if centre == 16 else odd[8]))
    return low, high[:4]


LOW, HIGH = impulse_responses()


def row_messages(even, odd):
    first = odd[0] + ALPHA * (even[0] + even[1])
    before = odd[-2] + ALPHA * (even[-2] + even[-1])
    p = odd[-1] + ALPHA * even[-1]
    q = p + GAMMA * (even[-1] + BETA * (before + p))
    return (p, q), (even[0], first)


def row_lift(even, odd, p, q, r, s):
    n = len(even)
    odd_one = [p + ALPHA * even[0]]
    odd_one += [odd[j] + ALPHA * (even[j] + (even[j + 1] if j + 1 < n else r)) for j in range(n)]
    even_two = [even[j] + BETA * (odd_one[j] + odd_one[j + 1]) for j in range(n)]
    even_two.append(r + BETA * (odd_one[n] + s))
    odd_three = [q + (ALPHA * (1.0 + GAMMA * BETA)) * even[0] + GAMMA * even_two[0]]
    odd_three += [odd_one[j + 1] + GAMMA * (even_two[j] + even_two[j + 1]) for j in range(n)]
    even_four = [even_two[j] + DELTA * (odd_three[j] + odd_three[j + 1]) for j in range(n)]
    return even_four, odd_three[1:]


def turn(value, amount):
    return pltpu.roll(value, amount % LANES, axis=1)


def column_lift(even, odd, step, lane, high_scale=1.0):
    n = len(even)

    def moved(tiles, distance):
        lanes = distance * step
        rolled = [turn(v, -lanes) for v in tiles]
        if distance > 0:
            return [jnp.where(lane >= LANES - lanes, rolled[(j + 1) % n], rolled[j]) for j in range(n)]
        return [jnp.where(lane < -lanes, rolled[j - 1], rolled[j]) for j in range(n)]

    even_at = {d: moved(even, d) for d in (-2, -1, 1, 2)}
    odd_at = {d: moved(odd, d) for d in (-2, -1, 1)}
    high_taps = [high_scale * tap for tap in HIGH]
    low, high = [], []
    for j in range(n):
        low.append(
            LOW[0] * even[j]
            + LOW[1] * (odd_at[-1][j] + odd[j])
            + LOW[2] * (even_at[-1][j] + even_at[1][j])
            + LOW[3] * (odd_at[-2][j] + odd_at[1][j])
            + LOW[4] * (even_at[-2][j] + even_at[2][j])
        )
        high.append(
            high_taps[0] * odd[j]
            + high_taps[1] * (even[j] + even_at[1][j])
            + high_taps[2] * (odd_at[-1][j] + odd_at[1][j])
            + high_taps[3] * (even_at[-1][j] + even_at[2][j])
        )
    return low, high


def split_pair(a, b, step, keep):
    even = [jnp.where(keep, u, turn(v, step)) for u, v in zip(a, b)]
    odd = [jnp.where(keep, turn(u, -step), v) for u, v in zip(a, b)]
    return even, odd


def join_pair(even, odd, step, keep):
    a = [jnp.where(keep, e, turn(o, step)) for e, o in zip(even, odd)]
    b = [jnp.where(keep, turn(e, -step), o) for e, o in zip(even, odd)]
    return a, b


def tap_values():
    root = math.sqrt(3.0)
    scale = 4.0 * math.sqrt(2.0)
    low = [(1.0 + root) / scale, (3.0 + root) / scale, (3.0 - root) / scale, (1.0 - root) / scale]
    return low, [low[3], -low[2], low[1], -low[0]]


def cutoff_pattern(pointer_ref, half):
    row = lax.broadcasted_iota(jnp.int32, (ROWS, LANES), 0)
    col = lax.broadcasted_iota(jnp.int32, (ROWS, LANES), 1)
    fine = 3 + 2 * (row % 2) + col % 2
    coarse = 2 * (row // 2 % 2) + col // 2 % 2
    band = jnp.where(row % 2 + col % 2 > 0, fine, coarse)
    power = jnp.zeros((ROWS, LANES), jnp.int32)
    for number in range(7):
        power = jnp.where(band == number, pointer_ref[7 * half + number], power)
    cutoff = jnp.full((ROWS, LANES), 0.05, jnp.float32)
    for bit in range(4):
        factor = 1.25 ** (2**bit)
        cutoff = jnp.where((power // 2**bit) % 2 == 1, cutoff * factor, cutoff)
    return cutoff


def kernel(
    tiles_count,
    x_hbm,
    flag_hbm,
    pointer_hbm,
    out_ref,
    pointer_ref,
    x_ref,
    flag_ref,
    field,
    aligned,
    to_next,
    to_prev,
    from_prev,
    from_next,
    window,
    hold,
    to_next2,
    to_prev2,
    from_prev2,
    from_next2,
    send,
    recv,
    levels,
    load_sem,
    edge_send,
    edge_recv,
    edge2_send,
    edge2_recv,
    block_send,
    block_recv,
    own_sem,
    ready,
):
    me = lax.axis_index("lev")
    row_block = lax.axis_index("tile")
    place, half = me // 2, lax.rem(me, 2)
    has_prev = row_block > 0
    has_next = row_block < tiles_count - 1
    seam_prev = lax.rem(row_block, CHAIN) == 0
    late_prev = jnp.logical_and(has_prev, seam_prev)
    early_prev = jnp.logical_and(has_prev, jnp.logical_not(seam_prev))
    seen_by_next = jnp.logical_and(has_next, lax.rem(row_block, CHAIN) == CHAIN - 1)
    row_1_first = lax.rem(row_block, CHAIN) == 1
    lane = lax.broadcasted_iota(jnp.int32, (ROWS, LANES), 1)
    lane_even = lane % 2 == 0
    lane_low = lane % 4 < 2
    nothing = jnp.zeros((ROWS, LANES), jnp.float32)

    barrier = pltpu.get_barrier_semaphore()
    for step in range(1, PARTS):
        pl.semaphore_signal(
            barrier,
            inc=1,
            device_id={"lev": lax.rem(me + step, PARTS)},
            device_id_type=MESH,
        )

    @pl.when(has_prev)
    def _():
        pl.semaphore_signal(
            barrier, inc=1, device_id={"tile": row_block - 1}, device_id_type=MESH
        )

    @pl.when(jnp.logical_and(has_next, jnp.logical_not(seen_by_next)))
    def _():
        pl.semaphore_signal(
            barrier, inc=1, device_id={"tile": row_block + 1}, device_id_type=MESH
        )

    loads = [
        pltpu.make_async_copy(x_hbm.at[level], x_ref.at[level], load_sem.at[level])
        for level in range(ROWS)
    ]
    loads.append(pltpu.make_async_copy(flag_hbm, flag_ref, load_sem.at[ROWS]))
    loads.append(pltpu.make_async_copy(pointer_hbm, pointer_ref, load_sem.at[ROWS + 1]))
    for load in loads:
        load.start()

    def clear(edge, edge2):
        def clear_window(k, _):
            for j in range(WIDE):
                edge[k, j, 0] = nothing
                edge[k, j, 1] = nothing
                edge2[k, j] = nothing
            return 0

        lax.fori_loop(0, WINDOWS, clear_window, 0)

    @pl.when(jnp.logical_not(has_prev))
    def _():
        clear(from_prev, from_prev2)

    @pl.when(jnp.logical_not(has_next))
    def _():
        clear(from_next, from_next2)

    field[pl.ds(0, GROUP), :] = jnp.zeros((GROUP, LANES), jnp.float32)
    field[pl.ds((PADDED - 2) * GROUP, 2 * GROUP), :] = jnp.zeros((2 * GROUP, LANES), jnp.float32)
    pl.semaphore_wait(
        barrier, PARTS - 1 + jnp.where(early_prev, 1, 0) + jnp.where(has_next, 1, 0)
    )

    @pl.when(seen_by_next)
    def _():
        pl.semaphore_signal(
            ready, inc=1, device_id={"tile": row_block + 1}, device_id_type=MESH
        )

    for load in loads:
        load.wait()

    whole = WIDTH // LANES
    rest = WIDTH - whole * LANES

    def load_tile(tile, _):
        columns = pl.ds(pl.multiple_of(tile * LANES, LANES), LANES)
        water = (1 - flag_ref[:, columns]).astype(jnp.float32)
        for level in range(ROWS):
            start = pl.multiple_of((tile + 1) * GROUP + level * ROWS, ROWS)
            field[pl.ds(start, ROWS), :] = x_ref[level, :, columns] * water
        return 0

    lax.fori_loop(0, whole, load_tile, 0)
    water = (1 - flag_ref[:, pl.ds(whole * LANES, rest)]).astype(jnp.float32)
    for level in range(ROWS):
        start = (whole + 1) * GROUP + level * ROWS
        field[pl.ds(start, ROWS), pl.ds(0, rest)] = (
            x_ref[level, :, pl.ds(whole * LANES, rest)] * water
        )

    def window_of(k):
        return lax.rem(place + 1 + k, WINDOWS)

    def edge_forward(k):
        return pltpu.make_async_remote_copy(
            src_ref=to_next.at[k],
            dst_ref=from_prev.at[k],
            send_sem=edge_send.at[0, k],
            recv_sem=edge_recv.at[0, k],
            device_id={"tile": row_block + 1},
            device_id_type=MESH,
        )

    def edge_backward(k):
        return pltpu.make_async_remote_copy(
            src_ref=to_prev.at[k],
            dst_ref=from_next.at[k],
            send_sem=edge_send.at[1, k],
            recv_sem=edge_recv.at[1, k],
            device_id={"tile": row_block - 1},
            device_id_type=MESH,
        )

    def edge2_forward(k):
        return pltpu.make_async_remote_copy(
            src_ref=to_next2.at[k],
            dst_ref=from_prev2.at[k],
            send_sem=edge2_send.at[0, k],
            recv_sem=edge2_recv.at[0, k],
            device_id={"tile": row_block + 1},
            device_id_type=MESH,
        )

    def edge2_backward(k):
        return pltpu.make_async_remote_copy(
            src_ref=to_prev2.at[k],
            dst_ref=from_next2.at[k],
            send_sem=edge2_send.at[1, k],
            recv_sem=edge2_recv.at[1, k],
            device_id={"tile": row_block - 1},
            device_id_type=MESH,
        )

    def block_copy(k, b, piece):
        lines = pl.ds(*PIECES[piece])
        return pltpu.make_async_remote_copy(
            src_ref=send.at[2 * k + b, lines],
            dst_ref=recv.at[me, lines],
            send_sem=block_send.at[piece, 2 * k + b],
            recv_sem=block_recv.at[piece, me],
            device_id={"lev": 2 * window_of(k) + b},
            device_id_type=MESH,
        )

    def from_source(source, piece):
        lines = pl.ds(*PIECES[piece])
        return pltpu.make_async_remote_copy(
            src_ref=send.at[0, lines],
            dst_ref=recv.at[source, lines],
            send_sem=block_send.at[piece, 0],
            recv_sem=block_recv.at[piece, source],
            device_id={"lev": source},
            device_id_type=MESH,
        )

    def own_copy(piece):
        lines = pl.ds(*PIECES[piece])
        return pltpu.make_async_copy(
            send.at[2 * (WINDOWS - 1) + half, lines], recv.at[me, lines], own_sem.at[piece]
        )

    def start_blocks(k, piece):
        for b in range(2):
            is_own = jnp.logical_and(k == WINDOWS - 1, half == b)

            @pl.when(jnp.logical_not(is_own))
            def _():
                block_copy(k, b, piece).start()

            @pl.when(is_own)
            def _():
                own_copy(piece).start()

    def put_row(k, row, tiles, first=False):
        at = ROW_AT[row]
        for j in range(FULL):
            send[2 * k, pl.ds(at + j * ROWS, ROWS), :] = tiles[j]
        rolled = [turn(tiles[j], -TAIL) for j in range(FULL, WIDE)]
        for j in range(FULL):
            send[2 * k + 1, pl.ds(at + j * ROWS, ROWS), :] = jnp.where(
                lane < LANES - TAIL, rolled[j], rolled[j + 1]
            )
        start = TAIL * TAIL_AT[row]
        lines = pl.ds(ODD_TAILS if row % 2 else EVEN_TAILS, ROWS)
        for b, tail in enumerate((tiles[FULL], rolled[FULL])):
            tail = turn(tail, start)
            if not first:
                mine = jnp.logical_and(lane >= start, lane < start + TAIL)
                tail = jnp.where(mine, tail, send[2 * k + b, lines, :])
            send[2 * k + b, lines, :] = tail

    def rows_of(k, j):
        start = (k * WIDE + j) * GROUP
        return [aligned[pl.ds(start + row, ROWS, stride=ROWS), :] for row in range(ROWS)]

    def edge_stage(k, _):
        w = window_of(k)
        first = (w * 2 * BLOCK) // LANES
        shift = w * 2 * BLOCK - first * LANES
        back = lax.rem(LANES - shift, LANES)
        inside = lane < LANES - shift
        halo, before = None, None
        for i in range(WIDE + 2):
            tile = [
                pltpu.roll(
                    field[pl.ds(pl.multiple_of((first + i) * GROUP + level * ROWS, ROWS), ROWS), :],
                    back,
                    axis=1,
                )
                for level in range(ROWS)
            ]
            if i > 0:
                moved = [jnp.where(inside, u, v) for u, v in zip(before, tile)]
                if i == 1:
                    halo = moved
                else:
                    if i == WIDE + 1:
                        moved = [
                            jnp.where(lane < LAST + HALO, u, v) for u, v in zip(moved, halo)
                        ]
                    for level in range(ROWS):
                        start = (k * WIDE + i - 2) * GROUP + level * ROWS
                        aligned[pl.ds(pl.multiple_of(start, ROWS), ROWS), :] = moved[level]
            before = tile
        for j in range(WIDE):
            rows = rows_of(k, j)
            forward, backward = row_messages(rows[0::2], rows[1::2])
            for i in range(2):
                to_next[k, j, i] = forward[i]
                to_prev[k, j, i] = backward[i]

        @pl.when(has_next)
        def _():
            edge_forward(k).start()

        @pl.when(early_prev)
        def _():
            edge_backward(k).start()

        return 0

    lax.fori_loop(0, WINDOWS, edge_stage, 0)

    def middle_row(k, j):
        rows = rows_of(k, j)
        return row_lift(rows[0::2], rows[1::2], *[nothing] * 4)[1][1]

    def middle_stage(pair, _):
        k = 2 * pair
        a = [middle_row(k, j) for j in range(WIDE)]
        b = [middle_row(k + 1, j) for j in range(WIDE)]
        even, odd = split_pair(a, b, 1, lane_even)
        even, odd = column_lift(even, odd, 2, lane, KAPPA * KAPPA)
        for n, row in enumerate(join_pair(even, odd, 1, lane_even)):
            put_row(k + n, 3, row, first=True)
            start_blocks(k + n, 0)
        return 0

    lax.fori_loop(0, WINDOWS // 2, middle_stage, 0)

    def wait_prev(k):
        @pl.when(has_prev)
        def _():
            edge_forward(k).wait_recv()

    def wait_next(k):
        @pl.when(has_next)
        def _():
            edge_backward(k).wait_recv()

    def row_1_stage(k):
        row_1 = []
        for j in range(WIDE):
            rows = rows_of(k, j)
            rest = [nothing] * 3
            row_1.append(row_lift(rows[0::2], rows[1::2], from_prev[k, j, 0], *rest)[1][0])
        even, odd = row_1, [turn(v, -1) for v in row_1]
        even, odd = column_lift(even, odd, 2, lane, KAPPA * KAPPA)
        put_row(k, 1, [jnp.where(lane_even, e, turn(o, 1)) for e, o in zip(even, odd)])
        start_blocks(k, 2)

    def rows_5_7_stage(k):
        row_5, row_7 = [], []
        for j in range(WIDE):
            rows = rows_of(k, j)
            edges = (nothing, nothing, from_next[k, j, 0], from_next[k, j, 1])
            odd = row_lift(rows[0::2], rows[1::2], *edges)[1]
            row_5.append(odd[2])
            row_7.append(odd[3])
        even, odd = split_pair(row_5, row_7, 1, lane_even)
        even, odd = column_lift(even, odd, 2, lane, KAPPA * KAPPA)
        row_5, row_7 = join_pair(even, odd, 1, lane_even)
        put_row(k, 5, row_5)
        put_row(k, 7, row_7)
        start_blocks(k, 1)

    def first_stage(k):
        w = window_of(k)
        for j in range(WIDE):
            rows = rows_of(k, j)
            even, _ = row_lift(
                rows[0::2],
                rows[1::2],
                from_prev[k, j, 0],
                from_prev[k, j, 1],
                from_next[k, j, 0],
                from_next[k, j, 1],
            )
            for i in range(4):
                window[i, j] = even[i]

        def split(a, b):
            tiles = [[window[i, j] for j in range(WIDE)] for i in (a, b)]
            return split_pair(*tiles, 1, lane_even)

        within = jnp.logical_or(
            lane < LAST,
            jnp.logical_or(
                jnp.logical_and(lane < LAST + HALO, w < WINDOWS - 1),
                jnp.logical_and(lane >= LAST + HALO, w > 0),
            ),
        )
        low_a, high_a = column_lift(*split(0, 2), 2, lane)
        low_b, high_b = column_lift(*split(1, 3), 2, lane)
        low_a[-1] = jnp.where(within, low_a[-1], 0.0)
        low_b[-1] = jnp.where(within, low_b[-1], 0.0)
        even, odd = split_pair(low_a, low_b, 2, lane_low)
        even, odd = column_lift(even, odd, 4, lane)
        low_a, low_b = join_pair(even, odd, 2, lane_low)
        c0, c2 = join_pair(low_a, high_a, 1, lane_even)
        c1, c3 = join_pair(low_b, high_b, 1, lane_even)
        for j in range(WIDE):
            for i, row in enumerate((c0, c1, c2, c3)):
                hold[k, i, j] = row[j]
            (p, q), (r, s) = row_messages([c0[j], c2[j]], [c1[j], c3[j]])
            to_next2[k, j] = jnp.where(lane_even, p, turn(q, 1))
            to_prev2[k, j] = jnp.where(lane_even, r, turn(s, 1))

        @pl.when(has_next)
        def _():
            edge2_forward(k).start()

        @pl.when(has_prev)
        def _():
            edge2_backward(k).start()

    square = KAPPA * KAPPA
    one = jnp.ones((ROWS, LANES), jnp.float32)
    scale_even = jnp.where(
        lane_even, jnp.where(lane_low, 1.0 / (square * square), 1.0 / square), one
    )
    scale_odd = jnp.where(jnp.logical_and(lane_even, lane_low), 1.0 / square, one)

    def second_stage(k):
        @pl.when(has_prev)
        def _():
            edge2_forward(k).wait_recv()

        @pl.when(has_next)
        def _():
            edge2_backward(k).wait_recv()

        rows = [[None] * WIDE for _ in range(4)]
        for j in range(WIDE):
            c = [hold[k, i, j] for i in range(4)]
            p = from_prev2[k, j]
            r = from_next2[k, j]
            even, odd = row_lift(c[0::2], c[1::2], p, turn(p, -1), r, turn(r, -1))
            for i in range(2):
                rows[2 * i][j] = jnp.where(lane_even, even[i], c[2 * i]) * scale_even
                rows[2 * i + 1][j] = jnp.where(lane_even, odd[i], c[2 * i + 1]) * scale_odd
        for i in range(4):
            put_row(k, 2 * i, rows[i], first=i == 0)
        start_blocks(k, 3)

    @pl.when(row_1_first)
    def _():
        def early_stage(k, _):
            wait_prev(k)
            row_1_stage(k)
            return 0

        lax.fori_loop(0, WINDOWS, early_stage, 0)

    @pl.when(seam_prev)
    def _():
        def early_stage(k, _):
            wait_next(k)
            rows_5_7_stage(k)
            return 0

        lax.fori_loop(0, WINDOWS, early_stage, 0)

    @pl.when(late_prev)
    def _():
        pl.semaphore_wait(ready, 1)

        def backward_stage(k, _):
            edge_backward(k).start()
            return 0

        lax.fori_loop(0, WINDOWS, backward_stage, 0)

    def stages(k, _):
        @pl.when(k < WINDOWS)
        def _():
            @pl.when(jnp.logical_not(row_1_first))
            def _():
                wait_prev(k)

            @pl.when(jnp.logical_not(seam_prev))
            def _():
                wait_next(k)

            first_stage(k)

            @pl.when(jnp.logical_not(row_1_first))
            def _():
                row_1_stage(k)

            @pl.when(jnp.logical_not(seam_prev))
            def _():
                rows_5_7_stage(k)

        @pl.when(k >= 4)
        def _():
            second_stage(k - 4)

        return 0

    lax.fori_loop(0, WINDOWS + 4, stages, 0)

    def spread(source):
        for row in range(ROWS):
            start = (source * ROWS + row) * SPAN * ROWS
            for j in range(FULL):
                levels[pl.ds(pl.multiple_of(start + j * ROWS, ROWS), ROWS), :] = recv[
                    source, pl.ds(ROW_AT[row] + j * ROWS, ROWS), :
                ]
            tail = recv[source, pl.ds(ODD_TAILS if row % 2 else EVEN_TAILS, ROWS), :]
            levels[pl.ds(pl.multiple_of(start + FULL * ROWS, ROWS), ROWS), :] = turn(
                tail, -TAIL * TAIL_AT[row]
            )

    low_taps, high_taps = tap_values()
    cutoffs = [cutoff_pattern(pointer_ref, part) for part in range(2)]

    def level_tile(source, level, j):
        start = source * ROWS * SPAN * ROWS + j * ROWS + level
        return levels[pl.ds(start, ROWS, stride=SPAN * ROWS), :]

    def put_pair(source, i, j, taken):
        for part, taps in enumerate((low_taps, high_taps)):
            value = taps[0] * taken[0]
            for tap in range(1, 4):
                value = value + taps[tap] * taken[tap]
            cutoff = cutoffs[part]
            value = value - jnp.minimum(jnp.maximum(value, -cutoff), cutoff)
            row = part * PARTS * ROWS // 2 + source * (ROWS // 2) + i
            if j == FULL:
                out_ref[row, :, pl.ds(FULL * LANES, TAIL)] = value[:, :TAIL]
            else:
                out_ref[row, :, pl.ds(j * LANES, LANES)] = value

    def within_source(source):
        spread(source)
        for j in range(SPAN):
            taken = [level_tile(source, level, j) for level in range(ROWS)]
            for i in range(ROWS // 2 - 1):
                put_pair(source, i, j, taken[2 * i : 2 * i + 4])

    def arrived(n, _):
        step = (n + 1) // 2
        source = 2 * lax.rem(place + WINDOWS - step, WINDOWS) + lax.rem(half + n, 2)

        @pl.when(n == 0)
        def _():
            for piece in range(len(PIECES)):
                own_copy(piece).wait()

        @pl.when(n > 0)
        def _():
            for piece in range(len(PIECES)):
                from_source(source, piece).wait_recv()

        within_source(source)
        return 0

    lax.fori_loop(0, PARTS, arrived, 0)

    def across_sources(source, _):
        after = lax.rem(source + 1, PARTS)
        for j in range(SPAN):
            taken = [level_tile(source, level, j) for level in (ROWS - 2, ROWS - 1)]
            taken += [level_tile(after, level, j) for level in range(2)]
            put_pair(source, ROWS // 2 - 1, j, taken)
        return 0

    lax.fori_loop(0, PARTS, across_sources, 0)

    def sent(k, _):
        @pl.when(has_next)
        def _():
            edge_forward(k).wait_send()
            edge2_forward(k).wait_send()

        @pl.when(has_prev)
        def _():
            edge_backward(k).wait_send()
            edge2_backward(k).wait_send()

        for b in range(2):

            @pl.when(jnp.logical_not(jnp.logical_and(k == WINDOWS - 1, half == b)))
            def _():
                for piece in range(len(PIECES)):
                    block_copy(k, b, piece).wait_send()

        return 0

    lax.fori_loop(0, WINDOWS, sent, 0)


def local(tiles_count, thermal_deviation, terrain_flag, frequency_share_limit_pointer):
    tile = (ROWS, LANES)
    vmem = lambda *shape: pltpu.VMEM(shape, jnp.float32)
    dma = pltpu.SemaphoreType.DMA
    return pl.pallas_call(
        functools.partial(kernel, tiles_count),
        out_shape=pltpu.VMEM((PARTS * ROWS, ROWS, BLOCK), jnp.float32),
        in_specs=[
            pl.BlockSpec(memory_space=pltpu.HBM),
            pl.BlockSpec(memory_space=pltpu.HBM),
            pl.BlockSpec(memory_space=pltpu.HBM),
        ],
        out_specs=pl.BlockSpec(memory_space=pltpu.VMEM),
        scratch_shapes=[
            pltpu.SMEM((14,), jnp.int32),
            vmem(ROWS, ROWS, WIDTH),
            pltpu.VMEM((ROWS, WIDTH), jnp.int32),
            vmem(PADDED * GROUP, LANES),
            vmem(WINDOWS * WIDE * GROUP, LANES),
            vmem(WINDOWS, WIDE, 2, *tile),
            vmem(WINDOWS, WIDE, 2, *tile),
            vmem(WINDOWS, WIDE, 2, *tile),
            vmem(WINDOWS, WIDE, 2, *tile),
            vmem(4, WIDE, *tile),
            vmem(WINDOWS, 4, WIDE, *tile),
            vmem(WINDOWS, WIDE, *tile),
            vmem(WINDOWS, WIDE, *tile),
            vmem(WINDOWS, WIDE, *tile),
            vmem(WINDOWS, WIDE, *tile),
            vmem(PARTS, MESSAGE, LANES),
            vmem(PARTS, MESSAGE, LANES),
            vmem(PARTS * ROWS * SPAN * ROWS, LANES),
            dma((ROWS + 2,)),
            dma((2, WINDOWS)),
            dma((2, WINDOWS)),
            dma((2, WINDOWS)),
            dma((2, WINDOWS)),
            dma((len(PIECES), PARTS)),
            dma((len(PIECES), PARTS)),
            dma((len(PIECES),)),
            pltpu.SemaphoreType.REGULAR,
        ],
        compiler_params=pltpu.CompilerParams(
            collective_id=0, has_side_effects=True, vmem_limit_bytes=40 * 1024 * 1024
        ),
    )(
        pltpu.with_memory_space_constraint(thermal_deviation, pltpu.HBM),
        pltpu.with_memory_space_constraint(terrain_flag, pltpu.HBM),
        pltpu.with_memory_space_constraint(frequency_share_limit_pointer, pltpu.HBM),
    )


def solution(mesh):
    placed = (P("lev", "tile", None), P("tile", None), P())
    return jax.shard_map(
        functools.partial(local, mesh.shape["tile"]),
        mesh=mesh,
        in_specs=placed,
        out_specs=P(None, "tile", "lev"),
        check_vma=False,
    )
```

```python
import functools
import math

import jax
import jax.numpy as jnp
import numpy as np
from jax import lax
from jax.experimental import pallas as pl
from jax.experimental.pallas import tpu as pltpu
from jax.sharding import PartitionSpec as P

ALPHA = -1.586134342
BETA = -0.05298011854
GAMMA = 0.8829110762
DELTA = 0.4435068522
KAPPA = 1.149604398

LANES = 128
ROWS = 8
WIDTH = 4320
PARTS = 8
BLOCK = WIDTH // PARTS
FULL = BLOCK // LANES
TAIL = BLOCK - FULL * LANES
SPAN = FULL + 1
WINDOWS = 4
WIDE = 9
LAST = 2 * BLOCK - (WIDE - 1) * LANES
HALO = (LANES - LAST) // 2
PADDED = 36
GROUP = ROWS * ROWS
ROW_LINES = FULL * ROWS
SLOTS = (3, 5, 7, 1, 0, 2, 4, 6)
ROW_AT = {row: i * ROW_LINES for i, row in enumerate(SLOTS)}
ODD_TAILS = ROWS * ROW_LINES
EVEN_TAILS = ODD_TAILS + ROWS
MESSAGE = EVEN_TAILS + ROWS
PIECES = (
    (0, ROW_LINES),
    (ROW_LINES, 2 * ROW_LINES),
    (3 * ROW_LINES, ROW_LINES),
    (4 * ROW_LINES, MESSAGE - 4 * ROW_LINES),
)
TAIL_AT = {row: row // 2 for row in range(ROWS)}
CHAIN = 8
MESH = pl.DeviceIdType.MESH


def impulse_responses():
    low, high = [], []
    for distance in range(5):
        for centre, taps in ((16, low), (17, high)):
            signal = np.zeros(34)
            signal[centre + distance] = 1.0
            even, odd = signal[0::2].copy(), signal[1::2].copy()
            odd[:-1] += ALPHA * (even[:-1] + even[1:])
            even[1:] += BETA * (odd[:-1] + odd[1:])
            odd[:-1] += GAMMA * (even[:-1] + even[1:])
            even[1:] += DELTA * (odd[:-1] + odd[1:])
            taps.append(float(even[8] if centre == 16 else odd[8]))
    return low, high[:4]


LOW, HIGH = impulse_responses()


def row_messages(even, odd):
    first = odd[0] + ALPHA * (even[0] + even[1])
    before = odd[-2] + ALPHA * (even[-2] + even[-1])
    p = odd[-1] + ALPHA * even[-1]
    q = p + GAMMA * (even[-1] + BETA * (before + p))
    return (p, q), (even[0], first)


def row_lift(even, odd, p, q, r, s):
    n = len(even)
    odd_one = [p + ALPHA * even[0]]
    odd_one += [odd[j] + ALPHA * (even[j] + (even[j + 1] if j + 1 < n else r)) for j in range(n)]
    even_two = [even[j] + BETA * (odd_one[j] + odd_one[j + 1]) for j in range(n)]
    even_two.append(r + BETA * (odd_one[n] + s))
    odd_three = [q + (ALPHA * (1.0 + GAMMA * BETA)) * even[0] + GAMMA * even_two[0]]
    odd_three += [odd_one[j + 1] + GAMMA * (even_two[j] + even_two[j + 1]) for j in range(n)]
    even_four = [even_two[j] + DELTA * (odd_three[j] + odd_three[j + 1]) for j in range(n)]
    return even_four, odd_three[1:]


def turn(value, amount):
    return pltpu.roll(value, amount % LANES, axis=1)


def column_lift(even, odd, step, lane, high_scale=1.0):
    n = len(even)

    def moved(tiles, distance):
        lanes = distance * step
        rolled = [turn(v, -lanes) for v in tiles]
        if distance > 0:
            return [jnp.where(lane >= LANES - lanes, rolled[(j + 1) % n], rolled[j]) for j in range(n)]
        return [jnp.where(lane < -lanes, rolled[j - 1], rolled[j]) for j in range(n)]

    even_at = {d: moved(even, d) for d in (-2, -1, 1, 2)}
    odd_at = {d: moved(odd, d) for d in (-2, -1, 1)}
    high_taps = [high_scale * tap for tap in HIGH]
    low, high = [], []
    for j in range(n):
        low.append(
            LOW[0] * even[j]
            + LOW[1] * (odd_at[-1][j] + odd[j])
            + LOW[2] * (even_at[-1][j] + even_at[1][j])
            + LOW[3] * (odd_at[-2][j] + odd_at[1][j])
            + LOW[4] * (even_at[-2][j] + even_at[2][j])
        )
        high.append(
            high_taps[0] * odd[j]
            + high_taps[1] * (even[j] + even_at[1][j])
            + high_taps[2] * (odd_at[-1][j] + odd_at[1][j])
            + high_taps[3] * (even_at[-1][j] + even_at[2][j])
        )
    return low, high


def split_pair(a, b, step, keep):
    even = [jnp.where(keep, u, turn(v, step)) for u, v in zip(a, b)]
    odd = [jnp.where(keep, turn(u, -step), v) for u, v in zip(a, b)]
    return even, odd


def join_pair(even, odd, step, keep):
    a = [jnp.where(keep, e, turn(o, step)) for e, o in zip(even, odd)]
    b = [jnp.where(keep, turn(e, -step), o) for e, o in zip(even, odd)]
    return a, b


def tap_values():
    root = math.sqrt(3.0)
    scale = 4.0 * math.sqrt(2.0)
    low = [(1.0 + root) / scale, (3.0 + root) / scale, (3.0 - root) / scale, (1.0 - root) / scale]
    return low, [low[3], -low[2], low[1], -low[0]]


def cutoff_pattern(pointer_ref, half):
    row = lax.broadcasted_iota(jnp.int32, (ROWS, LANES), 0)
    col = lax.broadcasted_iota(jnp.int32, (ROWS, LANES), 1)
    fine = 3 + 2 * (row % 2) + col % 2
    coarse = 2 * (row // 2 % 2) + col // 2 % 2
    band = jnp.where(row % 2 + col % 2 > 0, fine, coarse)
    power = jnp.zeros((ROWS, LANES), jnp.int32)
    for number in range(7):
        power = jnp.where(band == number, pointer_ref[7 * half + number], power)
    cutoff = jnp.full((ROWS, LANES), 0.05, jnp.float32)
    for bit in range(4):
        factor = 1.25 ** (2**bit)
        cutoff = jnp.where((power // 2**bit) % 2 == 1, cutoff * factor, cutoff)
    return cutoff


def kernel(
    tiles_count,
    x_hbm,
    flag_hbm,
    pointer_hbm,
    out_ref,
    pointer_ref,
    x_ref,
    flag_ref,
    field,
    aligned,
    to_next,
    to_prev,
    from_prev,
    from_next,
    window,
    hold,
    to_next2,
    to_prev2,
    from_prev2,
    from_next2,
    send,
    recv,
    levels,
    load_sem,
    edge_send,
    edge_recv,
    edge2_send,
    edge2_recv,
    block_send,
    block_recv,
    own_sem,
    ready,
):
    me = lax.axis_index("lev")
    row_block = lax.axis_index("tile")
    place, half = me // 2, lax.rem(me, 2)
    has_prev = row_block > 0
    has_next = row_block < tiles_count - 1
    seam_prev = lax.rem(row_block, CHAIN) == 0
    late_prev = jnp.logical_and(has_prev, seam_prev)
    early_prev = jnp.logical_and(has_prev, jnp.logical_not(seam_prev))
    seen_by_next = jnp.logical_and(has_next, lax.rem(row_block, CHAIN) == CHAIN - 1)
    row_1_first = lax.rem(row_block, CHAIN) == 1
    lane = lax.broadcasted_iota(jnp.int32, (ROWS, LANES), 1)
    lane_even = lane % 2 == 0
    lane_low = lane % 4 < 2
    nothing = jnp.zeros((ROWS, LANES), jnp.float32)

    barrier = pltpu.get_barrier_semaphore()
    for step in range(1, PARTS):
        pl.semaphore_signal(
            barrier,
            inc=1,
            device_id={"lev": lax.rem(me + step, PARTS)},
            device_id_type=MESH,
        )

    @pl.when(has_prev)
    def _():
        pl.semaphore_signal(
            barrier, inc=1, device_id={"tile": row_block - 1}, device_id_type=MESH
        )

    @pl.when(jnp.logical_and(has_next, jnp.logical_not(seen_by_next)))
    def _():
        pl.semaphore_signal(
            barrier, inc=1, device_id={"tile": row_block + 1}, device_id_type=MESH
        )

    loads = [
        pltpu.make_async_copy(x_hbm.at[level], x_ref.at[level], load_sem.at[level])
        for level in range(ROWS)
    ]
    loads.append(pltpu.make_async_copy(flag_hbm, flag_ref, load_sem.at[ROWS]))
    loads.append(pltpu.make_async_copy(pointer_hbm, pointer_ref, load_sem.at[ROWS + 1]))
    for load in loads:
        load.start()

    def clear(edge, edge2):
        def clear_window(k, _):
            for j in range(WIDE):
                edge[k, j, 0] = nothing
                edge[k, j, 1] = nothing
                edge2[k, j] = nothing
            return 0

        lax.fori_loop(0, WINDOWS, clear_window, 0)

    @pl.when(jnp.logical_not(has_prev))
    def _():
        clear(from_prev, from_prev2)

    @pl.when(jnp.logical_not(has_next))
    def _():
        clear(from_next, from_next2)

    field[pl.ds(0, GROUP), :] = jnp.zeros((GROUP, LANES), jnp.float32)
    field[pl.ds((PADDED - 2) * GROUP, 2 * GROUP), :] = jnp.zeros((2 * GROUP, LANES), jnp.float32)
    pl.semaphore_wait(
        barrier, PARTS - 1 + jnp.where(early_prev, 1, 0) + jnp.where(has_next, 1, 0)
    )

    @pl.when(seen_by_next)
    def _():
        pl.semaphore_signal(
            ready, inc=1, device_id={"tile": row_block + 1}, device_id_type=MESH
        )

    for load in loads:
        load.wait()

    whole = WIDTH // LANES
    rest = WIDTH - whole * LANES

    def load_tile(tile, _):
        columns = pl.ds(pl.multiple_of(tile * LANES, LANES), LANES)
        water = (1 - flag_ref[:, columns]).astype(jnp.float32)
        for level in range(ROWS):
            start = pl.multiple_of((tile + 1) * GROUP + level * ROWS, ROWS)
            field[pl.ds(start, ROWS), :] = x_ref[level, :, columns] * water
        return 0

    lax.fori_loop(0, whole, load_tile, 0)
    water = (1 - flag_ref[:, pl.ds(whole * LANES, rest)]).astype(jnp.float32)
    for level in range(ROWS):
        start = (whole + 1) * GROUP + level * ROWS
        field[pl.ds(start, ROWS), pl.ds(0, rest)] = (
            x_ref[level, :, pl.ds(whole * LANES, rest)] * water
        )

    def window_of(k):
        return lax.rem(place + 1 + k, WINDOWS)

    def edge_forward(k):
        return pltpu.make_async_remote_copy(
            src_ref=to_next.at[k],
            dst_ref=from_prev.at[k],
            send_sem=edge_send.at[0, k],
            recv_sem=edge_recv.at[0, k],
            device_id={"tile": row_block + 1},
            device_id_type=MESH,
        )

    def edge_backward(k):
        return pltpu.make_async_remote_copy(
            src_ref=to_prev.at[k],
            dst_ref=from_next.at[k],
            send_sem=edge_send.at[1, k],
            recv_sem=edge_recv.at[1, k],
            device_id={"tile": row_block - 1},
            device_id_type=MESH,
        )

    def edge2_forward(k):
        return pltpu.make_async_remote_copy(
            src_ref=to_next2.at[k],
            dst_ref=from_prev2.at[k],
            send_sem=edge2_send.at[0, k],
            recv_sem=edge2_recv.at[0, k],
            device_id={"tile": row_block + 1},
            device_id_type=MESH,
        )

    def edge2_backward(k):
        return pltpu.make_async_remote_copy(
            src_ref=to_prev2.at[k],
            dst_ref=from_next2.at[k],
            send_sem=edge2_send.at[1, k],
            recv_sem=edge2_recv.at[1, k],
            device_id={"tile": row_block - 1},
            device_id_type=MESH,
        )

    def block_copy(k, b, piece):
        lines = pl.ds(*PIECES[piece])
        return pltpu.make_async_remote_copy(
            src_ref=send.at[2 * k + b, lines],
            dst_ref=recv.at[me, lines],
            send_sem=block_send.at[piece, 2 * k + b],
            recv_sem=block_recv.at[piece, me],
            device_id={"lev": 2 * window_of(k) + b},
            device_id_type=MESH,
        )

    def from_source(source, piece):
        lines = pl.ds(*PIECES[piece])
        return pltpu.make_async_remote_copy(
            src_ref=send.at[0, lines],
            dst_ref=recv.at[source, lines],
            send_sem=block_send.at[piece, 0],
            recv_sem=block_recv.at[piece, source],
            device_id={"lev": source},
            device_id_type=MESH,
        )

    def own_copy(piece):
        lines = pl.ds(*PIECES[piece])
        return pltpu.make_async_copy(
            send.at[2 * (WINDOWS - 1) + half, lines], recv.at[me, lines], own_sem.at[piece]
        )

    def start_blocks(k, piece):
        for b in range(2):
            is_own = jnp.logical_and(k == WINDOWS - 1, half == b)

            @pl.when(jnp.logical_not(is_own))
            def _():
                block_copy(k, b, piece).start()

            @pl.when(is_own)
            def _():
                own_copy(piece).start()

    def put_row(k, row, tiles, first=False):
        at = ROW_AT[row]
        for j in range(FULL):
            send[2 * k, pl.ds(at + j * ROWS, ROWS), :] = tiles[j]
        rolled = [turn(tiles[j], -TAIL) for j in range(FULL, WIDE)]
        for j in range(FULL):
            send[2 * k + 1, pl.ds(at + j * ROWS, ROWS), :] = jnp.where(
                lane < LANES - TAIL, rolled[j], rolled[j + 1]
            )
        start = TAIL * TAIL_AT[row]
        lines = pl.ds(ODD_TAILS if row % 2 else EVEN_TAILS, ROWS)
        for b, tail in enumerate((tiles[FULL], rolled[FULL])):
            tail = turn(tail, start)
            if not first:
                mine = jnp.logical_and(lane >= start, lane < start + TAIL)
                tail = jnp.where(mine, tail, send[2 * k + b, lines, :])
            send[2 * k + b, lines, :] = tail

    def rows_of(k, j):
        start = (k * WIDE + j) * GROUP
        return [aligned[pl.ds(start + row, ROWS, stride=ROWS), :] for row in range(ROWS)]

    def edge_stage(k, _):
        w = window_of(k)
        first = (w * 2 * BLOCK) // LANES
        shift = w * 2 * BLOCK - first * LANES
        back = lax.rem(LANES - shift, LANES)
        inside = lane < LANES - shift
        halo, before = None, None
        for i in range(WIDE + 2):
            tile = [
                pltpu.roll(
                    field[pl.ds(pl.multiple_of((first + i) * GROUP + level * ROWS, ROWS), ROWS), :],
                    back,
                    axis=1,
                )
                for level in range(ROWS)
            ]
            if i > 0:
                moved = [jnp.where(inside, u, v) for u, v in zip(before, tile)]
                if i == 1:
                    halo = moved
                else:
                    if i == WIDE + 1:
                        moved = [
                            jnp.where(lane < LAST + HALO, u, v) for u, v in zip(moved, halo)
                        ]
                    for level in range(ROWS):
                        start = (k * WIDE + i - 2) * GROUP + level * ROWS
                        aligned[pl.ds(pl.multiple_of(start, ROWS), ROWS), :] = moved[level]
            before = tile
        for j in range(WIDE):
            rows = rows_of(k, j)
            forward, backward = row_messages(rows[0::2], rows[1::2])
            for i in range(2):
                to_next[k, j, i] = forward[i]
                to_prev[k, j, i] = backward[i]

        @pl.when(has_next)
        def _():
            edge_forward(k).start()

        @pl.when(early_prev)
        def _():
            edge_backward(k).start()

        return 0

    lax.fori_loop(0, WINDOWS, edge_stage, 0)

    def middle_row(k, j):
        rows = rows_of(k, j)
        return row_lift(rows[0::2], rows[1::2], *[nothing] * 4)[1][1]

    def middle_stage(pair, _):
        k = 2 * pair
        a = [middle_row(k, j) for j in range(WIDE)]
        b = [middle_row(k + 1, j) for j in range(WIDE)]
        even, odd = split_pair(a, b, 1, lane_even)
        even, odd = column_lift(even, odd, 2, lane, KAPPA * KAPPA)
        for n, row in enumerate(join_pair(even, odd, 1, lane_even)):
            put_row(k + n, 3, row, first=True)
            start_blocks(k + n, 0)
        return 0

    lax.fori_loop(0, WINDOWS // 2, middle_stage, 0)

    def wait_prev(k):
        @pl.when(has_prev)
        def _():
            edge_forward(k).wait_recv()

    def wait_next(k):
        @pl.when(has_next)
        def _():
            edge_backward(k).wait_recv()

    def row_1_stage(k):
        row_1 = []
        for j in range(WIDE):
            rows = rows_of(k, j)
            rest = [nothing] * 3
            row_1.append(row_lift(rows[0::2], rows[1::2], from_prev[k, j, 0], *rest)[1][0])
        even, odd = row_1, [turn(v, -1) for v in row_1]
        even, odd = column_lift(even, odd, 2, lane, KAPPA * KAPPA)
        put_row(k, 1, [jnp.where(lane_even, e, turn(o, 1)) for e, o in zip(even, odd)])
        start_blocks(k, 2)

    def rows_5_7_stage(k):
        row_5, row_7 = [], []
        for j in range(WIDE):
            rows = rows_of(k, j)
            edges = (nothing, nothing, from_next[k, j, 0], from_next[k, j, 1])
            odd = row_lift(rows[0::2], rows[1::2], *edges)[1]
            row_5.append(odd[2])
            row_7.append(odd[3])
        even, odd = split_pair(row_5, row_7, 1, lane_even)
        even, odd = column_lift(even, odd, 2, lane, KAPPA * KAPPA)
        row_5, row_7 = join_pair(even, odd, 1, lane_even)
        put_row(k, 5, row_5)
        put_row(k, 7, row_7)
        start_blocks(k, 1)

    def first_stage(k):
        w = window_of(k)
        for j in range(WIDE):
            rows = rows_of(k, j)
            even, _ = row_lift(
                rows[0::2],
                rows[1::2],
                from_prev[k, j, 0],
                from_prev[k, j, 1],
                from_next[k, j, 0],
                from_next[k, j, 1],
            )
            for i in range(4):
                window[i, j] = even[i]

        def split(a, b):
            tiles = [[window[i, j] for j in range(WIDE)] for i in (a, b)]
            return split_pair(*tiles, 1, lane_even)

        within = jnp.logical_or(
            lane < LAST,
            jnp.logical_or(
                jnp.logical_and(lane < LAST + HALO, w < WINDOWS - 1),
                jnp.logical_and(lane >= LAST + HALO, w > 0),
            ),
        )
        low_a, high_a = column_lift(*split(0, 2), 2, lane)
        low_b, high_b = column_lift(*split(1, 3), 2, lane)
        low_a[-1] = jnp.where(within, low_a[-1], 0.0)
        low_b[-1] = jnp.where(within, low_b[-1], 0.0)
        even, odd = split_pair(low_a, low_b, 2, lane_low)
        even, odd = column_lift(even, odd, 4, lane)
        low_a, low_b = join_pair(even, odd, 2, lane_low)
        c0, c2 = join_pair(low_a, high_a, 1, lane_even)
        c1, c3 = join_pair(low_b, high_b, 1, lane_even)
        for j in range(WIDE):
            for i, row in enumerate((c0, c1, c2, c3)):
                hold[k, i, j] = row[j]
            (p, q), (r, s) = row_messages([c0[j], c2[j]], [c1[j], c3[j]])
            to_next2[k, j] = jnp.where(lane_even, p, turn(q, 1))
            to_prev2[k, j] = jnp.where(lane_even, r, turn(s, 1))

        @pl.when(has_next)
        def _():
            edge2_forward(k).start()

        @pl.when(has_prev)
        def _():
            edge2_backward(k).start()

    square = KAPPA * KAPPA
    one = jnp.ones((ROWS, LANES), jnp.float32)
    scale_even = jnp.where(
        lane_even, jnp.where(lane_low, 1.0 / (square * square), 1.0 / square), one
    )
    scale_odd = jnp.where(jnp.logical_and(lane_even, lane_low), 1.0 / square, one)

    def second_stage(k):
        @pl.when(has_prev)
        def _():
            edge2_forward(k).wait_recv()

        @pl.when(has_next)
        def _():
            edge2_backward(k).wait_recv()

        rows = [[None] * WIDE for _ in range(4)]
        for j in range(WIDE):
            c = [hold[k, i, j] for i in range(4)]
            p = from_prev2[k, j]
            r = from_next2[k, j]
            even, odd = row_lift(c[0::2], c[1::2], p, turn(p, -1), r, turn(r, -1))
            for i in range(2):
                rows[2 * i][j] = jnp.where(lane_even, even[i], c[2 * i]) * scale_even
                rows[2 * i + 1][j] = jnp.where(lane_even, odd[i], c[2 * i + 1]) * scale_odd
        for i in range(4):
            put_row(k, 2 * i, rows[i], first=i == 0)
        start_blocks(k, 3)

    @pl.when(row_1_first)
    def _():
        def early_stage(k, _):
            wait_prev(k)
            row_1_stage(k)
            return 0

        lax.fori_loop(0, WINDOWS, early_stage, 0)

    @pl.when(seam_prev)
    def _():
        def early_stage(k, _):
            wait_next(k)
            rows_5_7_stage(k)
            return 0

        lax.fori_loop(0, WINDOWS, early_stage, 0)

    @pl.when(late_prev)
    def _():
        pl.semaphore_wait(ready, 1)

        def backward_stage(k, _):
            edge_backward(k).start()
            return 0

        lax.fori_loop(0, WINDOWS, backward_stage, 0)

    def stages(k, _):
        @pl.when(k < WINDOWS)
        def _():
            @pl.when(jnp.logical_not(row_1_first))
            def _():
                wait_prev(k)

            @pl.when(jnp.logical_not(seam_prev))
            def _():
                wait_next(k)

            first_stage(k)

            @pl.when(jnp.logical_not(row_1_first))
            def _():
                row_1_stage(k)

            @pl.when(jnp.logical_not(seam_prev))
            def _():
                rows_5_7_stage(k)

        @pl.when(k >= 4)
        def _():
            second_stage(k - 4)

        return 0

    lax.fori_loop(0, WINDOWS + 4, stages, 0)

    def spread(source):
        for row in range(ROWS):
            start = (source * ROWS + row) * SPAN * ROWS
            for j in range(FULL):
                levels[pl.ds(pl.multiple_of(start + j * ROWS, ROWS), ROWS), :] = recv[
                    source, pl.ds(ROW_AT[row] + j * ROWS, ROWS), :
                ]
            tail = recv[source, pl.ds(ODD_TAILS if row % 2 else EVEN_TAILS, ROWS), :]
            levels[pl.ds(pl.multiple_of(start + FULL * ROWS, ROWS), ROWS), :] = turn(
                tail, -TAIL * TAIL_AT[row]
            )

    low_taps, high_taps = tap_values()
    cutoffs = [cutoff_pattern(pointer_ref, part) for part in range(2)]

    def level_tile(source, level, j):
        start = source * ROWS * SPAN * ROWS + j * ROWS + level
        return levels[pl.ds(start, ROWS, stride=SPAN * ROWS), :]

    def put_pair(source, i, j, taken):
        for part, taps in enumerate((low_taps, high_taps)):
            value = taps[0] * taken[0]
            for tap in range(1, 4):
                value = value + taps[tap] * taken[tap]
            cutoff = cutoffs[part]
            value = value - jnp.minimum(jnp.maximum(value, -cutoff), cutoff)
            row = part * PARTS * ROWS // 2 + source * (ROWS // 2) + i
            if j == FULL:
                out_ref[row, :, pl.ds(FULL * LANES, TAIL)] = value[:, :TAIL]
            else:
                out_ref[row, :, pl.ds(j * LANES, LANES)] = value

    def within_source(source):
        spread(source)
        for j in range(SPAN):
            taken = [level_tile(source, level, j) for level in range(ROWS)]
            for i in range(ROWS // 2 - 1):
                put_pair(source, i, j, taken[2 * i : 2 * i + 4])

    def arrived(n, _):
        step = (n + 1) // 2
        source = 2 * lax.rem(place + WINDOWS - step, WINDOWS) + lax.rem(half + n, 2)

        @pl.when(n == 0)
        def _():
            for piece in range(len(PIECES)):
                own_copy(piece).wait()

        @pl.when(n > 0)
        def _():
            for piece in range(len(PIECES)):
                from_source(source, piece).wait_recv()

        within_source(source)
        return 0

    lax.fori_loop(0, PARTS, arrived, 0)

    def across_sources(source, _):
        after = lax.rem(source + 1, PARTS)
        for j in range(SPAN):
            taken = [level_tile(source, level, j) for level in (ROWS - 2, ROWS - 1)]
            taken += [level_tile(after, level, j) for level in range(2)]
            put_pair(source, ROWS // 2 - 1, j, taken)
        return 0

    lax.fori_loop(0, PARTS, across_sources, 0)

    def sent(k, _):
        @pl.when(has_next)
        def _():
            edge_forward(k).wait_send()
            edge2_forward(k).wait_send()

        @pl.when(has_prev)
        def _():
            edge_backward(k).wait_send()
            edge2_backward(k).wait_send()

        for b in range(2):

            @pl.when(jnp.logical_not(jnp.logical_and(k == WINDOWS - 1, half == b)))
            def _():
                for piece in range(len(PIECES)):
                    block_copy(k, b, piece).wait_send()

        return 0

    lax.fori_loop(0, WINDOWS, sent, 0)


def local(tiles_count, thermal_deviation, terrain_flag, frequency_share_limit_pointer):
    tile = (ROWS, LANES)
    vmem = lambda *shape: pltpu.VMEM(shape, jnp.float32)
    dma = pltpu.SemaphoreType.DMA
    return pl.pallas_call(
        functools.partial(kernel, tiles_count),
        out_shape=pltpu.VMEM((PARTS * ROWS, ROWS, BLOCK), jnp.float32),
        in_specs=[
            pl.BlockSpec(memory_space=pltpu.HBM),
            pl.BlockSpec(memory_space=pltpu.HBM),
            pl.BlockSpec(memory_space=pltpu.HBM),
        ],
        out_specs=pl.BlockSpec(memory_space=pltpu.VMEM),
        scratch_shapes=[
            pltpu.SMEM((14,), jnp.int32),
            vmem(ROWS, ROWS, WIDTH),
            pltpu.VMEM((ROWS, WIDTH), jnp.int32),
            vmem(PADDED * GROUP, LANES),
            vmem(WINDOWS * WIDE * GROUP + ROWS, LANES),
            vmem(WINDOWS, WIDE, 2, *tile),
            vmem(WINDOWS, WIDE, 2, *tile),
            vmem(WINDOWS, WIDE, 2, *tile),
            vmem(WINDOWS, WIDE, 2, *tile),
            vmem(4, WIDE, *tile),
            vmem(WINDOWS, 4, WIDE, *tile),
            vmem(WINDOWS, WIDE, *tile),
            vmem(WINDOWS, WIDE, *tile),
            vmem(WINDOWS, WIDE, *tile),
            vmem(WINDOWS, WIDE, *tile),
            vmem(PARTS, MESSAGE, LANES),
            vmem(PARTS, MESSAGE, LANES),
            vmem((PARTS * ROWS + 1) * SPAN * ROWS, LANES),
            dma((ROWS + 2,)),
            dma((2, WINDOWS)),
            dma((2, WINDOWS)),
            dma((2, WINDOWS)),
            dma((2, WINDOWS)),
            dma((len(PIECES), PARTS)),
            dma((len(PIECES), PARTS)),
            dma((len(PIECES),)),
            pltpu.SemaphoreType.REGULAR,
        ],
        compiler_params=pltpu.CompilerParams(
            collective_id=0, has_side_effects=True, vmem_limit_bytes=40 * 1024 * 1024
        ),
    )(
        pltpu.with_memory_space_constraint(thermal_deviation, pltpu.HBM),
        pltpu.with_memory_space_constraint(terrain_flag, pltpu.HBM),
        pltpu.with_memory_space_constraint(frequency_share_limit_pointer, pltpu.HBM),
    )


def solution(mesh):
    placed = (P("lev", "tile", None), P("tile", None), P())
    return jax.shard_map(
        functools.partial(local, mesh.shape["tile"]),
        mesh=mesh,
        in_specs=placed,
        out_specs=P(None, "tile", "lev"),
        check_vma=False,
    )
```
